256 devices in a mesh: slab: 128 (over z, y, x_lo, core), grp: 2 (over x_hi).
Axes of the slice: x: 4 (x_hi: 2, x_lo: 2; x = x_hi * 2 + x_lo), y: 4, z: 8, core: 2. Of those that a mesh axis runs over, the one named last changes fastest.
Arguments:
- base_index: int32 [3, 131072], P(None, ('slab', 'grp')), may hold values from 0 to 511, as said below
- fraction: float32 [3, 131072], P(None, ('slab', 'grp')), may hold values from 0 to 1
- charge: float32 [131072], P(('slab', 'grp')), may hold values from -4 to 4
- atom_count: int32 [256], P(('slab', 'grp')), may hold values from 256 to 512, as said below
- owner_index: int32 [32768], P(('slab', 'grp')), may hold values from 0 to 127, as said below
- neighbour: int32 [32, 32768], P(None, ('slab', 'grp')), may hold values from 0 to 767, as said below
- influence: float32 [256, 512, 512], P('grp', 'slab'), may hold values from 1 to 300
- layer_one: bfloat16 [128, 240], replicated, may hold values from -0.5 to 0.5
- bias_one: float32 [240], replicated, may hold values from -3 to 3
- layer_two: bfloat16 [240, 240], replicated, may hold values from -0.375 to 0.375
- bias_two: float32 [240], replicated, may hold values from -3 to 3
- layer_out: bfloat16 [240, 3], replicated, may hold values from -0.375 to 0.375
- bias_out: float32 [3], replicated, may hold values from -3 to 3
Outputs:
- atom_force: float32 [3, 131072], P(None, ('slab', 'grp'))
- potential: float32 [256, 512, 512], P(('slab', 'grp'))
The draws below stay inside these ranges and needn't reach their ends.
Inputs may be any that keep to these rules, and one draw needn't show every extreme that they name: `base_index`: row 0 is an x base cell below 512, row 1 a y base cell below 512, row 2 a base plane below 1 within the device. The first 128 atoms of every device fall into 16 groups by position modulo 16; in each group the x and y bases of all devices lie within 4 cells, periodically, of a common point. `atom_count`: slots at or beyond a device's count are padding. One device uses all 512 slots and one uses half of them. `owner_index`: on each device the centroids name each of the atoms 0 .. 127 once. `neighbour`: indices into the device's extended list (first 128 atoms of the device before, its own 512 atoms, first 128 atoms of the device after). Every slot names one of the first 128 atoms of one of the three devices, in the owner's group (same position modulo 16), never the owner itself; slots may repeat.
All inputs are finite; a program needn't handle non-finite values.
Results may differ from the reference program's by a relative error of at most 0.0076.
The reference program's roundings to bfloat16 on the way (of `potential_b`) count: a program that leaves them out, or rounds other values in their place, can miss the bound.
Values may be sent and summed in bfloat16 or wider, within the bound.
No kernel may reach another device: no remote copies, remote signals or barrier semaphores. Data moves between devices by JAX's collectives and lax.ppermute only.
A program may use at most 64 MiB of HBM per device.

```python
import math
import jax
import jax.numpy as jnp
from jax import lax

NX = 512
NY = 512
CZ = 1
ATOMS_DEV = 512
NEIGH = 32
HID = 240
NCL = 16
SPREAD = 4
SLABS = 256
NZ = 256
CENT_DEV = 128
RIM = 128
DESC = 128
NATOMS = 131072
N_SLAB = 128
N_GRP = 2


def owner_table(key):
    device_keys = jax.random.split(jax.random.fold_in(key, 21), SLABS)
    return jax.vmap(lambda single: jax.random.permutation(single, CENT_DEV))(device_keys)


def draw_base_index(key, part):
    total_rows = ATOMS_DEV * SLABS
    limits = jnp.array([[NX], [NY]], jnp.int32)
    centre = jax.random.randint(jax.random.fold_in(key, 11), (2, NCL), 0, limits)
    position = jnp.arange(total_rows) % ATOMS_DEV
    cluster = position % NCL
    jitter = jax.random.randint(jax.random.fold_in(key, 12), (2, total_rows), -SPREAD, SPREAD + 1)
    clustered = (centre[:, cluster] + jitter) % limits
    scattered = jax.random.randint(jax.random.fold_in(key, 13), (2, total_rows), 0, limits)
    plane_xy = jnp.where(position[None, :] < RIM, clustered, scattered)
    plane_z = jax.random.randint(jax.random.fold_in(key, 14), (1, total_rows), 0, CZ)
    return jnp.concatenate([plane_xy, plane_z], axis=0).astype(jnp.int32)


def draw_atom_count(key, part):
    counts = jax.random.randint(jax.random.fold_in(key, 41), (SLABS,), ATOMS_DEV // 2, ATOMS_DEV + 1)
    chosen_spots = jax.random.permutation(jax.random.fold_in(key, 42), SLABS)
    counts = counts.at[chosen_spots[0]].set(ATOMS_DEV).at[chosen_spots[1]].set(ATOMS_DEV // 2)
    return counts.astype(jnp.int32)


def draw_owner_index(key, part):
    return owner_table(key).reshape(-1).astype(jnp.int32)


def draw_neighbour(key, part):
    owners = owner_table(key)
    cluster = owners % NCL
    owner_rank = owners // NCL
    per_group = RIM // NCL
    grid_shape = (NEIGH, SLABS, CENT_DEV)
    source_side = jax.random.randint(jax.random.fold_in(key, 31), grid_shape, 0, 3)
    pick_rank = jax.random.randint(jax.random.fold_in(key, 32), grid_shape, 0, per_group)
    pick_local = jax.random.randint(jax.random.fold_in(key, 33), grid_shape, 0, per_group - 1)
    pick_local = pick_local + (pick_local >= owner_rank[None]).astype(jnp.int32)
    region_start = jnp.where(source_side == 0, 0, jnp.where(source_side == 1, RIM, RIM + ATOMS_DEV))
    chosen = jnp.where(source_side == 1, pick_local, pick_rank)
    result = region_start + cluster[None] + NCL * chosen
    return result.reshape(NEIGH, SLABS * CENT_DEV).astype(jnp.int32)


def level_of(rng, shape, shards, least, largest):
    level = 1.0
    for dim, parts in shards:
        steps = jax.random.uniform(jax.random.fold_in(jax.random.fold_in(rng, 6), dim), (parts,), jnp.float32, least / len(shards), largest / len(shards))
        level = level * jnp.repeat(jnp.exp(steps), shape[dim] // parts).reshape((-1,) + (1,) * (len(shape) - 1 - dim))
    return level


def centred(own_key, extent, deviation, bound, shards=(), kind=jnp.bfloat16):
    loudness = level_of(own_key, extent, shards, -0.22, 0.18) if shards else 1.0
    values = jax.random.normal(own_key, extent, jnp.float32) * deviation * loudness
    return jnp.minimum(jnp.maximum(values, -bound), bound).astype(kind)


def setup_inputs(seed: int = 0) -> dict:
    key_of = jax.random.split(jax.random.key(seed), 14)
    return {
        "base_index": draw_base_index(jax.random.fold_in(key_of[13], 71), 0),
        "fraction": jnp.clip(1.0 * jax.random.uniform(key_of[1], (3, NATOMS), jnp.float32) ** level_of(key_of[1], (3, NATOMS), ((1, 256),), -0.2, 0.2), 0.0, 1.0),
        "charge": centred(key_of[2], (NATOMS,), 1.0, 4.0, ((0, 256),), jnp.float32),
        "atom_count": draw_atom_count(jax.random.fold_in(key_of[13], 71), 0),
        "owner_index": draw_owner_index(jax.random.fold_in(key_of[13], 71), 0),
        "neighbour": draw_neighbour(jax.random.fold_in(key_of[13], 71), 0),
        "influence": jnp.clip(jnp.exp(math.log(300.0) - 5.7037825 * jax.random.uniform(key_of[6], (NZ, NX, NY), jnp.float32) ** level_of(key_of[6], (NZ, NX, NY), ((0, 2), (1, 128)), -0.2, 0.2)), 1.0, 300.0),
        "layer_one": centred(key_of[7], (DESC, HID), DESC ** -0.5, 0.5),
        "bias_one": centred(key_of[8], (HID,), 0.5, 3.0, (), jnp.float32),
        "layer_two": centred(key_of[9], (HID, HID), HID ** -0.5, 0.375),
        "bias_two": centred(key_of[10], (HID,), 0.5, 3.0, (), jnp.float32),
        "layer_out": centred(key_of[11], (HID, 3), HID ** -0.5, 0.375),
        "bias_out": centred(key_of[12], (3,), 0.5, 3.0, (), jnp.float32),
    }


DISPLACE_MAX = 1.0
RADIUS = 4.0
CENTROID_CHARGE = -2.0

def spline(offset):
    size = jnp.abs(offset)
    inner = 2.0 / 3.0 - size * size + 0.5 * size * size * size
    outer = (2.0 - size) ** 3 / 6.0
    return jnp.where(size < 1.0, inner, jnp.where(size < 2.0, outer, 0.0 * size))

def spline_slope(offset):
    size = jnp.abs(offset)
    inner = (-2.0 * size + 1.5 * size * size) * jnp.sign(offset)
    outer = -0.5 * (2.0 - size) ** 2 * jnp.sign(offset)
    return jnp.where(size < 1.0, inner, jnp.where(size < 2.0, outer, 0.0 * size))

def wrap_int(values, period):
    return jnp.where(values >= period // 2, values - period, jnp.where(values < -(period // 2), values + period, values))

def features(displace):
    scale = lax.rsqrt(1.0 + (displace[0] ** 2 + displace[1] ** 2 + displace[2] ** 2) / (RADIUS * RADIUS))
    return jnp.stack([scale, scale * displace[0] / RADIUS, scale * displace[1] / RADIUS, scale * displace[2] / RADIUS], axis=-1)

def fitting(inputs, layer_one, bias_one, layer_two, bias_two, layer_out, bias_out):
    pre_one = jnp.dot(inputs.astype(jnp.bfloat16), layer_one, preferred_element_type=jnp.float32) + bias_one
    hidden_one = jnp.tanh(pre_one)
    pre_two = jnp.dot(hidden_one.astype(jnp.bfloat16), layer_two, preferred_element_type=jnp.float32) + bias_two
    hidden_two = jnp.tanh(pre_two) + hidden_one
    raw_out = jnp.dot(hidden_two.astype(jnp.bfloat16), layer_out, preferred_element_type=jnp.float32) + bias_out
    tanh_out = jnp.tanh(raw_out)
    return (DISPLACE_MAX * tanh_out, (hidden_one, pre_two, tanh_out))

def fitting_back(pull, saved, layer_one, layer_two, layer_out):
    hidden_one, pre_two, tanh_out = saved
    grad_out = pull * (DISPLACE_MAX * (1.0 - tanh_out * tanh_out))
    grad_two = jnp.dot(grad_out.astype(jnp.bfloat16), layer_out.T, preferred_element_type=jnp.float32)
    tanh_two = jnp.tanh(pre_two)
    grad_pre = grad_two * (1.0 - tanh_two * tanh_two)
    grad_one = jnp.dot(grad_pre.astype(jnp.bfloat16), layer_two.T, preferred_element_type=jnp.float32) + grad_two
    grad_first = grad_one * (1.0 - hidden_one * hidden_one)
    return jnp.dot(grad_first.astype(jnp.bfloat16), layer_one.T, preferred_element_type=jnp.float32)

def hartley(values, axis_index):
    spectrum = jnp.fft.fft(values, axis=axis_index)
    return jnp.real(spectrum) - jnp.imag(spectrum)

def rounded(values):
    return lax.optimization_barrier(values.astype(jnp.bfloat16)).astype(values.dtype)

def scatter_rows(row_index, row_values, width):
    return jnp.zeros((3, width), row_values.dtype).at[:, row_index].add(row_values)

def reference(base_index, fraction, charge, atom_count, owner_index, neighbour, influence, layer_one, bias_one, layer_two, bias_two, layer_out, bias_out):
    slab_count = N_SLAB * N_GRP
    mesh_depth = CZ * slab_count
    atom_rows = ATOMS_DEV
    real_type = fraction.dtype
    base_int = base_index.reshape(3, slab_count, atom_rows)
    frac = fraction.reshape(3, slab_count, atom_rows)
    present = (jnp.arange(atom_rows)[None, :] < atom_count[:, None]).astype(real_type)
    atom_charge = charge.reshape(slab_count, atom_rows) * present
    base_real = base_int.astype(real_type)
    lift = jnp.array([0.0, 0.0, float(CZ)], dtype=real_type)[:, None, None]
    ext_base = jnp.concatenate([jnp.roll(base_real[:, :, :RIM], 1, axis=1) - lift, base_real, jnp.roll(base_real[:, :, :RIM], -1, axis=1) + lift], axis=2)
    ext_frac = jnp.concatenate([jnp.roll(frac[:, :, :RIM], 1, axis=1), frac, jnp.roll(frac[:, :, :RIM], -1, axis=1)], axis=2)
    own_rows = owner_index.reshape(slab_count, CENT_DEV)
    own_base = jnp.take_along_axis(base_real, own_rows[None], axis=2)
    own_frac = jnp.take_along_axis(frac, own_rows[None], axis=2)
    near_rows = neighbour.reshape(NEIGH, slab_count, CENT_DEV).transpose(1, 0, 2).reshape(slab_count, NEIGH * CENT_DEV)
    near_base = jnp.take_along_axis(ext_base, near_rows[None], axis=2).reshape(3, slab_count, NEIGH, CENT_DEV)
    near_frac = jnp.take_along_axis(ext_frac, near_rows[None], axis=2).reshape(3, slab_count, NEIGH, CENT_DEV)
    int_part = near_base - own_base[:, :, None, :]
    int_part = jnp.stack([wrap_int(int_part[0], NX), wrap_int(int_part[1], NY), int_part[2]])
    displace = int_part + (near_frac - own_frac[:, :, None, :])
    feature_rows, feature_back = jax.vjp(features, displace)
    inputs = feature_rows.transpose(0, 2, 1, 3).reshape(slab_count * CENT_DEV, 4 * NEIGH)
    shifted, saved = fitting(inputs, layer_one, bias_one, layer_two, bias_two, layer_out, bias_out)
    shifted = shifted.reshape(slab_count, CENT_DEV, 3).transpose(2, 0, 1)
    part_int = jnp.concatenate([base_int, jnp.take_along_axis(base_int, own_rows[None], axis=2)], axis=2)
    part_frac = jnp.concatenate([frac, own_frac + shifted], axis=2)
    part_charge = jnp.concatenate([atom_charge, jnp.full((slab_count, CENT_DEV), CENTROID_CHARGE, real_type)], axis=1)
    offsets = jnp.arange(-2, 4)
    stencil = offsets.astype(real_type)[None, None, None, :] - part_frac[..., None]
    weights = spline(stencil)
    slopes = spline_slope(stencil)
    plane_base = (jnp.arange(slab_count) * CZ)[:, None] + part_int[2]
    z_cells = (plane_base[..., None] + offsets) % mesh_depth
    x_cells = (part_int[0][..., None] + offsets) % NX
    y_cells = (part_int[1][..., None] + offsets) % NY
    charge_z = part_charge[..., None] * weights[2]
    scaled_x = rounded(charge_z[..., :, None] * weights[0][..., None, :])
    weight_y_b = rounded(weights[1])
    contrib = scaled_x[..., :, None, :] * weight_y_b[..., None, :, None]
    z_index = z_cells[..., :, None, None]
    y_index = y_cells[..., None, :, None]
    x_index = x_cells[..., None, None, :]
    density = jnp.zeros((mesh_depth, NX, NY), real_type).at[z_index, x_index, y_index].add(contrib)
    spectrum = hartley(hartley(hartley(density, 2), 1), 0)
    potential = hartley(hartley(hartley(influence * spectrum, 0), 1), 2) / float(NX * NY * mesh_depth)
    potential_b = rounded(potential)
    near_field = potential_b[z_index, x_index, y_index]
    weight_x_b = rounded(weights[0])
    slope_x_b = rounded(slopes[0])
    sum_value = lax.optimization_barrier(jnp.sum(near_field * weight_x_b[..., None, None, :], axis=-1))
    sum_slope = lax.optimization_barrier(jnp.sum(near_field * slope_x_b[..., None, None, :], axis=-1))
    probed = lax.optimization_barrier(jnp.sum(sum_value * weights[1][..., None, :], axis=-1))
    along_x = lax.optimization_barrier(jnp.sum(sum_slope * weights[1][..., None, :], axis=-1))
    along_y = lax.optimization_barrier(jnp.sum(sum_value * slopes[1][..., None, :], axis=-1))
    pushed = part_charge[None] * jnp.stack([lax.optimization_barrier(jnp.sum(along_x * weights[2], axis=-1)), lax.optimization_barrier(jnp.sum(along_y * weights[2], axis=-1)), lax.optimization_barrier(jnp.sum(probed * slopes[2], axis=-1))])
    pull = pushed[:, :, atom_rows:]
    grad_inputs = fitting_back(pull.transpose(1, 2, 0).reshape(-1, 3), saved, layer_one, layer_two, layer_out)
    cotangent = grad_inputs.reshape(slab_count, CENT_DEV, NEIGH, 4).transpose(0, 2, 1, 3)
    grad_displace, = feature_back(cotangent)
    ext_width = 2 * RIM + atom_rows
    ext_force = jax.vmap(lambda row_index, row_values: scatter_rows(row_index, row_values, ext_width), in_axes=(0, 1), out_axes=1)(near_rows, grad_displace.reshape(3, slab_count, NEIGH * CENT_DEV))
    owner_term = pull - lax.optimization_barrier(jnp.sum(grad_displace, axis=2))
    ext_force = ext_force + jax.vmap(lambda row_index, row_values: scatter_rows(row_index, row_values, ext_width), in_axes=(0, 1), out_axes=1)(RIM + own_rows, owner_term)
    local_force = ext_force[:, :, RIM:RIM + atom_rows]
    rim_in = jnp.roll(ext_force[:, :, RIM + atom_rows:], 1, axis=1) + jnp.roll(ext_force[:, :, :RIM], -1, axis=1)
    local_force = local_force.at[:, :, :RIM].add(rim_in)
    atom_force = (pushed[:, :, :atom_rows] + local_force).reshape(3, slab_count * atom_rows)
    return (atom_force, potential)
```

```python
import functools

import jax
import jax.numpy as jnp
import ml_dtypes
import numpy as np
from jax import lax
from jax.experimental import pallas as pl
from jax.experimental.pallas import tpu as pltpu
from jax.sharding import PartitionSpec as P

NX = 512
NY = 512
NZ = 256
NEIGH = 32
HID = 256
CENTROID_CHARGE = -2.0
BF = jnp.bfloat16
F32 = jnp.float32
NEAR = tuple(range(-4, 4))
ROWS = 24
MIB = 1024 * 1024


def cas_pair(row_ids, column_ids, period):
    angle = 2.0 * np.pi / period * (np.outer(row_ids, column_ids) % period)
    table = np.cos(angle) + np.sin(angle)
    high = table.astype(ml_dtypes.bfloat16)
    low = (table - high.astype(np.float64)).astype(ml_dtypes.bfloat16)
    return high, low


def spline(offset):
    size = jnp.abs(offset)
    inner = 2.0 / 3.0 - size * size + 0.5 * size * size * size
    rest = 2.0 - size
    outer = rest * rest * rest * (1.0 / 6.0)
    return jnp.where(size < 1.0, inner, jnp.where(size < 2.0, outer, 0.0))


def spline_slope(offset):
    size = jnp.abs(offset)
    sign = jnp.where(offset > 0.0, 1.0, jnp.where(offset < 0.0, -1.0, 0.0))
    inner = (-2.0 * size + 1.5 * size * size) * sign
    rest = 2.0 - size
    outer = -0.5 * rest * rest * sign
    return jnp.where(size < 1.0, inner, jnp.where(size < 2.0, outer, 0.0))


def wrapped(values):
    return jnp.where(
        values >= 256.0, values - 512.0, jnp.where(values < -256.0, values + 512.0, values)
    )


def dot(left, right):
    return jnp.dot(left, right, preferred_element_type=F32)


def split(values):
    high = values.astype(BF)
    low = (values - high.astype(F32)).astype(BF)
    return high, low


def pack_kernel(count_ref, base_ref, frac_ref, charge_ref, owner_ref, near_ref, out_ref):
    for k in range(4):
        lanes = slice(128 * k, 128 * (k + 1))
        out_ref[k : k + 1, :] = base_ref[0:1, lanes].astype(F32)
        out_ref[4 + k : 5 + k, :] = base_ref[1:2, lanes].astype(F32)
        for c in range(3):
            out_ref[8 + 4 * c + k : 9 + 4 * c + k, :] = frac_ref[c : c + 1, lanes]
        slot = lax.broadcasted_iota(jnp.int32, (1, 128), 1) + 128 * k
        out_ref[20 + k : 21 + k, :] = jnp.where(
            slot < count_ref[0], charge_ref[k : k + 1, :], 0.0
        )
    owner = owner_ref[...]
    near = near_ref[...]
    side = jnp.where(near < 128, 0, jnp.where(near < 256, 8, 16))
    code = side + (((owner >> 4) - ((near & 127) >> 4)) & 7)
    atom = lax.broadcasted_iota(jnp.int32, (128, 128), 0)
    chosen = jnp.where(atom == owner, 1.0, 0.0).astype(BF)
    out_ref[24:56, :] = lax.dot_general(
        code.astype(F32).astype(BF), chosen, (((1,), (1,)), ((), ())), preferred_element_type=F32
    )


def spread_kernel(
    p0, p1, p2, p3, p4, p5, p6, p7,
    w1_ref, b1_ref, w2_ref, b2_ref, wo_ref, bo_ref, hh_ref, hl_ref,
    out_ref, part_ref, h1_ref, t2_ref, to_ref,
    code_s, feat_s, in_s, xin_s, cell_s, wgt_s, sx_s, wy_s,
):
    pays = (p0, p1, p2, p3, p4, p5, p6, p7)
    rim = [jnp.concatenate([ref[r : r + 1, :] for ref in pays], axis=0) for r in (0, 4, 8, 12, 16)]
    for i in range(8):
        code_s[:, i, :] = pays[i][24:56, :]
    for j in range(8):
        turned = [pltpu.roll(v, 16 * j, 1) if j else v for v in rim]
        for s in (-1, 0, 1):
            cand = [pltpu.roll(v, (-s) % 8, 0) if s else v for v in turned]
            dx = wrapped(cand[0] - rim[0]) + (cand[2] - rim[2])
            dy = wrapped(cand[1] - rim[1]) + (cand[3] - rim[3])
            dz = float(s) + (cand[4] - rim[4])
            scale = lax.rsqrt(1.0 + (dx * dx + dy * dy + dz * dz) * (1.0 / 16.0))
            c = (s + 1) * 8 + j
            feat_s[c, 0] = scale
            feat_s[c, 1] = scale * dx * 0.25
            feat_s[c, 2] = scale * dy * 0.25
            feat_s[c, 3] = scale * dz * 0.25

    def choose(block, carry):
        codes = [code_s[block * 4 + m] for m in range(4)]
        held = [[jnp.zeros((8, 128), F32) for _ in range(4)] for _ in range(4)]
        for c in range(24):
            feats = [feat_s[c, f] for f in range(4)]
            for m in range(4):
                mask = codes[m] == float(c)
                for f in range(4):
                    held[m][f] = jnp.where(mask, feats[f], held[m][f])
        for m in range(4):
            for f in range(4):
                in_s[(block * 4 + m) * 4 + f] = held[m][f]
        return carry

    lax.fori_loop(0, 8, choose, 0)
    for i in range(1, 7):
        xin_s[:, (i - 1) * 128 : i * 128] = in_s[:, i, :].astype(BF)
    h1 = jnp.tanh(dot(w1_ref[...], xin_s[...]) + b1_ref[...])
    t2 = jnp.tanh(dot(w2_ref[...], h1.astype(BF)) + b2_ref[...])
    to = jnp.tanh(dot(wo_ref[...], (t2 + h1).astype(BF)) + bo_ref[...])
    h1_ref[...] = h1[:, 256:640]
    t2_ref[...] = t2[:, 256:640]
    to_ref[...] = to[:, 256:640]
    for n, i in enumerate((2, 3, 4, 5)):
        rows = slice(4 * n, 4 * n + 4)
        for c in range(4):
            part_ref[c, rows, :] = pays[i][4 * c : 4 * c + 4, :]
        part_ref[4, rows, :] = float(4 - i) - pays[i][16:20, :]
        part_ref[5, rows, :] = pays[i][20:24, :]
    for i in range(1, 7):
        row = slice(15 + i, 16 + i)
        lanes = slice((i - 1) * 128, i * 128)
        part_ref[0, row, :] = pays[i][0:1, :]
        part_ref[1, row, :] = pays[i][4:5, :]
        part_ref[2, row, :] = pays[i][8:9, :] + to[0:1, lanes]
        part_ref[3, row, :] = pays[i][12:13, :] + to[1:2, lanes]
        part_ref[4, row, :] = float(4 - i) - (pays[i][16:17, :] + to[2:3, lanes])
        part_ref[5, row, :] = jnp.full((1, 128), CENTROID_CHARGE, F32)
    part_ref[:, 22:24, :] = jnp.zeros((6, 2, 128), F32)

    charge_z = part_ref[5] * spline(part_ref[4])
    for axis in range(2):
        cells, offsets = stencil(part_ref[axis], part_ref[2 + axis])
        for k in range(4):
            value = spline(offsets[k])
            cell_s[axis * 4 + k] = cells[k]
            wgt_s[axis * 4 + k] = charge_z * value if axis == 0 else value

    def tables(row, carry):
        lanes = pl.ds(pl.multiple_of(row * 128, 128), 128)
        for axis, table in ((0, sx_s), (1, wy_s)):
            cells = [cell_s[axis * 4 + k, pl.ds(row, 1), :] for k in range(4)]
            values = [wgt_s[axis * 4 + k, pl.ds(row, 1), :] for k in range(4)]
            for part in range(16):
                here = lax.broadcasted_iota(jnp.int32, (32, 128), 0).astype(F32) + 32.0 * part
                found = jnp.zeros((32, 128), F32)
                for k in range(4):
                    found = jnp.where(here == cells[k], values[k], found)
                table[32 * part : 32 * part + 32, lanes] = found.astype(BF)
        return carry

    lax.fori_loop(0, 22, tables, 0)
    density = lax.dot_general(
        sx_s[...], wy_s[...], (((1,), (1,)), ((), ())), preferred_element_type=F32
    )
    hh, hl = hh_ref[...], hl_ref[...]
    high, low = split(density)
    inner = dot(high, hh) + dot(low, hh) + dot(high, hl)
    high, low = split(inner)
    spectrum = dot(hh, high) + dot(hh, low) + dot(hl, high)
    lower = lax.broadcasted_iota(jnp.int32, (64, 8, 128), 1) < 4
    for g in range(2):
        tile0 = spectrum[:, 256 * g : 256 * g + 128].reshape(64, 8, 128)
        tile1 = spectrum[:, 256 * g + 128 : 256 * g + 256].reshape(64, 8, 128)
        even = jnp.where(lower, tile0, pltpu.roll(tile1, 4, 1))
        odd = jnp.where(lower, pltpu.roll(tile0, 4, 1), tile1)
        out_ref[:, 0, 8 * g : 8 * g + 8, :] = even.astype(BF)
        out_ref[:, 1, 8 * g : 8 * g + 8, :] = odd.astype(BF)


def stencil(base, frac):
    whole = jnp.floor(frac)
    cells, offsets = [], []
    for k in range(4):
        step = whole + float(k - 1)
        cell = base + step
        cell = jnp.where(cell < 0.0, cell + 512.0, jnp.where(cell >= 512.0, cell - 512.0, cell))
        cells.append(cell)
        offsets.append(step - frac)
    return cells, offsets


def depth_kernel(x_ref, infl_ref, fh_ref, fl_ref, ih_ref, il_ref, out_ref, wide_s, xb_s, back_s):
    wide_s[...] = x_ref[...].astype(F32)
    for r in range(8):
        lanes = slice(128 * r, 128 * r + 128)
        xb_s[0:128, lanes] = wide_s[:, r, :].astype(BF)
        xb_s[128:256, lanes] = wide_s[:, 8 + r, :].astype(BF)
    for r in range(0, 8, 2):
        lanes = slice(128 * r, 128 * r + 256)
        xb = xb_s[:, lanes]
        spectrum = dot(fh_ref[...], xb) + dot(fl_ref[...], xb)
        weight = jnp.concatenate([infl_ref[r], infl_ref[r + 1]], axis=1)
        high, low = split(spectrum * weight)
        back = dot(ih_ref[...], high) + dot(il_ref[...], high) + dot(ih_ref[...], low)
        for t in range(2):
            column = back[:, 128 * t : 128 * t + 128]
            back_s[:, r + t, :] = column[0:128]
            back_s[:, 8 + r + t, :] = column[128:256]
    out_ref[...] = back_s[...].astype(BF)


def probe_kernel(
    y_ref, part_ref, hh_ref, hl_ref,
    pot_ref, o0, o1, o2, o3, o4, o5, o6, o7,
    r_s, field_s, cell_s, wgt_s, wx_s, vs_s, push_s,
):
    outs = (o0, o1, o2, o3, o4, o5, o6, o7)
    lower = lax.broadcasted_iota(jnp.int32, (64, 8, 128), 1) < 4
    for g in range(2):
        even = y_ref[:, 0, 8 * g : 8 * g + 8, :].astype(F32)
        odd = y_ref[:, 1, 8 * g : 8 * g + 8, :].astype(F32)
        tile0 = jnp.where(lower, even, pltpu.roll(odd, 4, 1))
        tile1 = jnp.where(lower, pltpu.roll(even, 4, 1), odd)
        r_s[:, 256 * g : 256 * g + 128] = tile0.reshape(512, 128).astype(BF)
        r_s[:, 256 * g + 128 : 256 * g + 256] = tile1.reshape(512, 128).astype(BF)
    hh, hl = hh_ref[...], hl_ref[...]
    inner = dot(hh, r_s[...]) + dot(hl, r_s[...])
    high, low = split(inner)
    potential = (dot(high, hh) + dot(low, hh) + dot(high, hl)) * (1.0 / 67108864.0)
    pot_ref[0] = potential
    field_s[...] = potential.T.astype(BF)

    for axis in range(2):
        cells, offsets = stencil(part_ref[axis], part_ref[2 + axis])
        for k in range(4):
            cell_s[axis * 4 + k] = cells[k]
            wgt_s[axis * 4 + k] = spline(offsets[k])
            wgt_s[8 + axis * 4 + k] = spline_slope(offsets[k])

    def probe(row, carry):
        row_at = pl.ds(row, 1)
        cells = [cell_s[k, row_at, :] for k in range(4)]
        values = [wgt_s[k, row_at, :] for k in range(4)]
        slopes = [wgt_s[8 + k, row_at, :] for k in range(4)]
        for part in range(16):
            here = lax.broadcasted_iota(jnp.int32, (32, 128), 0).astype(F32) + 32.0 * part
            found = jnp.zeros((32, 128), F32)
            sloped = jnp.zeros((32, 128), F32)
            for k in range(4):
                mask = here == cells[k]
                found = jnp.where(mask, values[k], found)
                sloped = jnp.where(mask, slopes[k], sloped)
            wx_s[32 * part : 32 * part + 32, 0:128] = found.astype(BF)
            wx_s[32 * part : 32 * part + 32, 128:256] = sloped.astype(BF)
        vs_s[...] = dot(field_s[...], wx_s[...])
        cells = [cell_s[4 + k, row_at, :] for k in range(4)]
        values = [wgt_s[4 + k, row_at, :] for k in range(4)]
        slopes = [wgt_s[12 + k, row_at, :] for k in range(4)]
        probed = jnp.zeros((8, 128), F32)
        along_x = jnp.zeros((8, 128), F32)
        along_y = jnp.zeros((8, 128), F32)
        for part in range(64):
            rows = slice(8 * part, 8 * part + 8)
            here = lax.broadcasted_iota(jnp.int32, (8, 128), 0).astype(F32) + 8.0 * part
            found = jnp.zeros((8, 128), F32)
            sloped = jnp.zeros((8, 128), F32)
            for k in range(4):
                mask = here == cells[k]
                found = jnp.where(mask, values[k], found)
                sloped = jnp.where(mask, slopes[k], sloped)
            value = vs_s[rows, 0:128]
            slope = vs_s[rows, 128:256]
            probed = probed + value * found
            along_x = along_x + slope * found
            along_y = along_y + value * sloped
        push_s[0, row_at, :] = jnp.sum(along_x, axis=0, keepdims=True)
        push_s[1, row_at, :] = jnp.sum(along_y, axis=0, keepdims=True)
        push_s[2, row_at, :] = jnp.sum(probed, axis=0, keepdims=True)
        return carry

    lax.fori_loop(0, 22, probe, 0)
    charge = part_ref[5]
    charge_z = charge * spline(part_ref[4])
    charge_slope = charge * spline_slope(part_ref[4])
    push = [
        push_s[0] * charge_z,
        push_s[1] * charge_z,
        push_s[2] * charge_slope,
    ]
    for i in range(8):
        outs[i][...] = jnp.zeros((ROWS, 128), F32)
        for c in range(3):
            if 2 <= i <= 5:
                outs[i][4 * c : 4 * c + 4, :] = push[c][4 * (i - 2) : 4 * (i - 2) + 4]
            for n in range(3):
                source = i - 1 + n
                if 1 <= source <= 6:
                    outs[i][12 + 3 * c + n : 13 + 3 * c + n, :] = push[c][15 + source : 16 + source]


def force_kernel(
    s0, s1, s2, s3, s4, s5, s6, s7, before_ref, own_ref, after_ref,
    h1_ref, t2_ref, to_ref, w1_ref, w2_ref, wo_ref, out_ref, gin_s,
):
    total = s0[...] + s1[...] + s2[...] + s3[...] + s4[...] + s5[...] + s6[...] + s7[...]
    pull = [
        jnp.concatenate([total[12 + 3 * c + n : 13 + 3 * c + n] for n in range(3)], axis=1)
        for c in range(3)
    ]
    to = to_ref[...]
    pulls = jnp.concatenate(pull + [jnp.zeros((5, 384), F32)], axis=0)
    g_out = pulls * (1.0 - to * to)
    g_two = dot(wo_ref[...], g_out.astype(BF))
    t2, h1 = t2_ref[...], h1_ref[...]
    g_pre = g_two * (1.0 - t2 * t2)
    g_one = dot(w2_ref[...], g_pre.astype(BF)) + g_two
    gin_s[...] = dot(w1_ref[...], (g_one * (1.0 - h1 * h1)).astype(BF))
    pays = (before_ref, own_ref, after_ref)
    turn = lax.broadcasted_iota(jnp.int32, (8, 128), 0).astype(F32)

    def rims(ref):
        return [ref[r : r + 1, :] for r in (0, 4, 8, 12, 16)]

    def rolled(row):
        return jnp.concatenate([pltpu.roll(row, 16 * j, 1) if j else row for j in range(8)], axis=0)

    own_rim = rims(own_ref)
    turned = [[rolled(row) for row in rims(ref)] for ref in pays]
    force = [total[4 * c : 4 * c + 1] for c in range(3)]
    owner_sum = [jnp.zeros((8, 128), F32) for _ in range(3)]
    for n, s in ((0, 1), (1, -1), (1, 0), (1, 1), (2, -1)):
        owner = rims(pays[n])
        cand = turned[n + s]
        dx = wrapped(cand[0] - owner[0]) + (cand[2] - owner[2])
        dy = wrapped(cand[1] - owner[1]) + (cand[3] - owner[3])
        dz = float(s) + (cand[4] - owner[4])
        scale = lax.rsqrt(1.0 + (dx * dx + dy * dy + dz * dz) * (1.0 / 16.0))
        lanes = slice(128 * n, 128 * n + 128)
        mine = turn + float(8 * (s + 1))
        cots = [jnp.zeros((8, 128), F32) for _ in range(4)]
        for m in range(NEIGH):
            mask = pays[n][24 + m : 25 + m, :] == mine
            for f in range(4):
                cots[f] = cots[f] + jnp.where(mask, gin_s[4 * m + f : 4 * m + f + 1, lanes], 0.0)
        along = cots[0] + (cots[1] * dx + cots[2] * dy + cots[3] * dz) * 0.25
        common = along * (scale * scale * scale) * (-1.0 / 16.0)
        moved = [
            common * dx + cots[1] * scale * 0.25,
            common * dy + cots[2] * scale * 0.25,
            common * dz + cots[3] * scale * 0.25,
        ]
        if n == 1:
            owner_sum = [owner_sum[c] + moved[c] for c in range(3)]
        if n + s == 1:
            for c in range(3):
                for j in range(8):
                    row = moved[c][j : j + 1]
                    force[c] = force[c] + (pltpu.roll(row, (-16 * j) % 128, 1) if j else row)
    for c in range(3):
        own = force[c] + pull[c][:, 128:256] - jnp.sum(owner_sum[c], axis=0, keepdims=True)
        out_ref[c : c + 1, 0:128] = own
        for k in range(1, 4):
            out_ref[c : c + 1, 128 * k : 128 * k + 128] = total[4 * c + k : 4 * c + k + 1]


VM = pl.BlockSpec(memory_space=pltpu.VMEM)


def call(kernel, inputs, outs, scratch=(), limit=40, first=VM, flops=0):
    return pl.pallas_call(
        kernel,
        out_shape=outs,
        in_specs=[first] + [VM] * (len(inputs) - 1),
        out_specs=jax.tree.map(lambda _: VM, outs),
        scratch_shapes=list(scratch),
        compiler_params=pltpu.CompilerParams(vmem_limit_bytes=limit * MIB),
        cost_estimate=pl.CostEstimate(flops=flops, bytes_accessed=4 * MIB, transcendentals=0),
    )(*inputs)


def shape(*dims, dtype=F32):
    return jax.ShapeDtypeStruct(dims, dtype)


def body(
    base_index,
    fraction,
    charge,
    atom_count,
    owner_index,
    neighbour,
    influence,
    layer_one,
    bias_one,
    layer_two,
    bias_two,
    layer_out,
    bias_out,
):
    both = ("slab", "grp")
    devices = 256
    group = lax.axis_index("grp")

    def from_device(value, step):
        pairs = [(source, (source - step) % devices) for source in range(devices)]
        return lax.ppermute(value, both, pairs)

    plane_high, plane_low = cas_pair(np.arange(NX), np.arange(NX), NX)
    split_z = np.concatenate([np.arange(0, NZ, 2), np.arange(1, NZ, 2)])
    fore_high, fore_low = cas_pair(np.arange(NZ), split_z, NZ)
    back_high, back_low = cas_pair(split_z, np.arange(NZ), NZ)
    hh, hl = jnp.asarray(plane_high), jnp.asarray(plane_low)

    with jax.named_scope("pack"):
        payload = call(
            pack_kernel,
            (
                atom_count,
                base_index,
                fraction,
                charge.reshape(4, 128),
                owner_index.reshape(1, 128),
                neighbour,
            ),
            shape(56, 128),
            first=pl.BlockSpec(memory_space=pltpu.SMEM),
            limit=8,
        )
    with jax.named_scope("particles_in"):
        pays = [payload if step == 0 else from_device(payload, step) for step in NEAR]

    with jax.named_scope("influence_swap"):
        kept = lax.dynamic_slice_in_dim(influence, group * 256, 256, axis=2)
        given = lax.dynamic_slice_in_dim(influence, (1 - group) * 256, 256, axis=2)
        taken = lax.ppermute(given, "grp", [(0, 1), (1, 0)])
        infl = jnp.concatenate(
            [jnp.where(group == 0, kept, taken), jnp.where(group == 0, taken, kept)], axis=0
        )
        infl = infl.reshape(NZ, 4, 2, 128).transpose(2, 1, 0, 3).reshape(8, NZ, 128)

    pad = HID - layer_one.shape[1]
    one = jnp.pad(layer_one, ((0, 0), (0, pad)))
    two = jnp.pad(layer_two, ((0, pad), (0, pad)))
    out = jnp.pad(layer_out, ((0, pad), (0, 5)))
    b1 = jnp.pad(bias_one, (0, pad)).reshape(HID, 1)
    b2 = jnp.pad(bias_two, (0, pad)).reshape(HID, 1)
    bo = jnp.pad(bias_out, (0, 5)).reshape(8, 1)

    with jax.named_scope("spread"):
        columns, part, h1, t2, to = call(
            spread_kernel,
            (*pays, one.T, b1, two.T, b2, out.T, bo, hh, hl),
            (
                shape(64, 2, 16, 128, dtype=BF),
                shape(6, ROWS, 128),
                shape(HID, 384),
                shape(HID, 384),
                shape(8, 384),
            ),
            (
                pltpu.VMEM((NEIGH, 8, 128), F32),
                pltpu.VMEM((24, 4, 8, 128), F32),
                pltpu.VMEM((128, 8, 128), F32),
                pltpu.VMEM((128, 768), BF),
                pltpu.VMEM((8, ROWS, 128), F32),
                pltpu.VMEM((8, ROWS, 128), F32),
                pltpu.VMEM((NX, 22 * 128), BF),
                pltpu.VMEM((NY, 22 * 128), BF),
            ),
            flops=4_000_000_000,
        )
    with jax.named_scope("to_columns"):
        columns = lax.all_to_all(columns.reshape(256, 8, 128), both, 0, 0, tiled=True)
    with jax.named_scope("depth"):
        rows = call(
            depth_kernel,
            (
                columns.reshape(128, 16, 128),
                infl,
                jnp.asarray(fore_high),
                jnp.asarray(fore_low),
                jnp.asarray(back_high),
                jnp.asarray(back_low),
            ),
            shape(128, 16, 128, dtype=BF),
            (
                pltpu.VMEM((128, 16, 128), F32),
                pltpu.VMEM((NZ, 1024), BF),
                pltpu.VMEM((128, 16, 128), F32),
            ),
            flops=800_000_000,
        )
    with jax.named_scope("to_planes"):
        rows = lax.all_to_all(rows.reshape(256, 8, 128), both, 0, 0, tiled=True)
    with jax.named_scope("probe"):
        potential, *pushes = call(
            probe_kernel,
            (rows.reshape(64, 2, 16, 128), part, hh, hl),
            (shape(1, NX, NY),) + (shape(ROWS, 128),) * 8,
            (
                pltpu.VMEM((NX, NY), BF),
                pltpu.VMEM((NY, NX), BF),
                pltpu.VMEM((8, ROWS, 128), F32),
                pltpu.VMEM((16, ROWS, 128), F32),
                pltpu.VMEM((NX, 256), BF),
                pltpu.VMEM((NY, 256), F32),
                pltpu.VMEM((3, ROWS, 128), F32),
            ),
            flops=5_000_000_000,
        )
    with jax.named_scope("pushes_out"):
        sums = [
            push if step == 0 else from_device(push, -step) for step, push in zip(NEAR, pushes)
        ]
    with jax.named_scope("force"):
        force = call(
            force_kernel,
            (*sums, pays[3], pays[4], pays[5], h1, t2, to, one, two, out),
            shape(3, 512),
            (pltpu.VMEM((128, 384), F32),),
            limit=16,
        )
    return force, potential


def solution(mesh):
    return jax.shard_map(
        body,
        mesh=mesh,
        in_specs=(
            P(None, ("slab", "grp")),
            P(None, ("slab", "grp")),
            P(("slab", "grp")),
            P(("slab", "grp")),
            P(("slab", "grp")),
            P(None, ("slab", "grp")),
            P("grp", "slab", None),
            P(),
            P(),
            P(),
            P(),
            P(),
            P(),
        ),
        out_specs=(P(None, ("slab", "grp")), P(("slab", "grp"), None, None)),
        check_vma=False,
    )
```

```python
import functools

import jax
import jax.numpy as jnp
import ml_dtypes
import numpy as np
from jax import lax
from jax.experimental import pallas as pl
from jax.experimental.pallas import tpu as pltpu
from jax.sharding import PartitionSpec as P

NX = 512
NY = 512
NZ = 256
NEIGH = 32
HID = 240
CENTROID_CHARGE = -2.0
BF = jnp.bfloat16
F32 = jnp.float32
ROWS = 24
NEAR = tuple(range(-4, 4))
MIB = 1024 * 1024


def cas_pair(row_ids, column_ids, period):
    angle = 2.0 * np.pi / period * (np.outer(row_ids, column_ids) % period)
    table = np.cos(angle) + np.sin(angle)
    high = table.astype(ml_dtypes.bfloat16)
    low = (table - high.astype(np.float64)).astype(ml_dtypes.bfloat16)
    return high, low


def spline(offset):
    size = jnp.abs(offset)
    inner = 2.0 / 3.0 - size * size + 0.5 * size * size * size
    rest = 2.0 - size
    outer = rest * rest * rest * (1.0 / 6.0)
    return jnp.where(size < 1.0, inner, jnp.where(size < 2.0, outer, 0.0))


def spline_slope(offset):
    size = jnp.abs(offset)
    sign = jnp.where(offset > 0.0, 1.0, jnp.where(offset < 0.0, -1.0, 0.0))
    inner = (-2.0 * size + 1.5 * size * size) * sign
    rest = 2.0 - size
    outer = -0.5 * rest * rest * sign
    return jnp.where(size < 1.0, inner, jnp.where(size < 2.0, outer, 0.0))


def wrapped(values):
    return jnp.where(
        values >= 256.0, values - 512.0, jnp.where(values < -256.0, values + 512.0, values)
    )


def dot(left, right):
    return jnp.dot(left, right, preferred_element_type=F32)


def dot_first(left, right):
    return lax.dot_general(left, right, (((0,), (0,)), ((), ())), preferred_element_type=F32)


def split(values):
    high = values.astype(BF)
    low = (values - high.astype(F32)).astype(BF)
    return high, low


def fetch(pairs, sems, first=0):
    copies = [
        pltpu.make_async_copy(source, target, sems.at[first + n])
        for n, (source, target) in enumerate(pairs)
    ]
    for copy in copies:
        copy.start()
    return copies


def pack_kernel(
    count_ref, base_at, frac_at, charge_at, owner_at, near_at,
    out_ref, base_ref, frac_ref, charge_ref, owner_ref, near_ref, sems,
):
    arrays = (
        (base_at, base_ref), (frac_at, frac_ref), (charge_at, charge_ref),
        (owner_at, owner_ref), (near_at, near_ref),
    )
    copies = [pltpu.make_async_copy(a, b, sems.at[n]) for n, (a, b) in enumerate(arrays)]
    for copy in copies:
        copy.start()
    for copy in copies:
        copy.wait()
    for k in range(4):
        lanes = slice(128 * k, 128 * (k + 1))
        out_ref[k : k + 1, :] = base_ref[0:1, lanes].astype(F32)
        out_ref[4 + k : 5 + k, :] = base_ref[1:2, lanes].astype(F32)
        for c in range(3):
            out_ref[8 + 4 * c + k : 9 + 4 * c + k, :] = frac_ref[c : c + 1, lanes]
        slot = lax.broadcasted_iota(jnp.int32, (1, 128), 1) + 128 * k
        out_ref[20 + k : 21 + k, :] = jnp.where(
            slot < count_ref[0], charge_ref[k : k + 1, :], 0.0
        )
    owner = owner_ref[...]
    near = near_ref[...]
    side = jnp.where(near < 128, 0, jnp.where(near < 256, 8, 16))
    code = side + (((owner >> 4) - ((near & 127) >> 4)) & 7)
    atom = lax.broadcasted_iota(jnp.int32, (128, 128), 0)
    chosen = jnp.where(atom == owner, 1.0, 0.0).astype(BF)
    out_ref[24:56, :] = lax.dot_general(
        code.astype(F32).astype(BF), chosen, (((1,), (1,)), ((), ())), preferred_element_type=F32
    )


def atom_rows(part_ref, first, pay, plane):
    rows = slice(first, first + 4)
    for c in range(4):
        part_ref[c, rows, :] = pay(4 * c, 4 * c + 4)
    part_ref[4, rows, :] = plane - pay(16, 20)
    part_ref[5, rows, :] = pay(20, 24)


def stencil(base, frac):
    whole = jnp.floor(frac)
    cells, offsets = [], []
    for k in range(4):
        step = whole + float(k - 1)
        cell = base + step
        cell = jnp.where(cell < 0.0, cell + 512.0, jnp.where(cell >= 512.0, cell - 512.0, cell))
        cells.append(cell)
        offsets.append(step - frac)
    return cells, offsets


def densities(part_ref, cell_s, wgt_s, tables, total_s):
    charge_z = part_ref[5] * spline(part_ref[4])
    for axis in range(2):
        cells, offsets = stencil(part_ref[axis], part_ref[2 + axis])
        for k in range(4):
            value = spline(offsets[k])
            cell_s[axis * 4 + k] = cells[k]
            wgt_s[axis * 4 + k] = charge_z * value if axis == 0 else value
    place = lax.broadcasted_iota(jnp.int32, (16, 128), 0).astype(F32)
    zero = jnp.zeros((16, 128), BF)

    def fill(row, axis, table, lane):
        cells = [cell_s[axis * 4 + k, row : row + 1, :] for k in range(4)]
        blocks = [jnp.floor(cell * (1.0 / 16.0)) for cell in cells]
        here, there = jnp.zeros((16, 128), F32), jnp.zeros((16, 128), F32)
        for k in range(4):
            value = wgt_s[axis * 4 + k, row : row + 1, :]
            at = jnp.where(blocks[k] == blocks[0], cells[k] - 16.0 * blocks[k], -1.0)
            past = jnp.where(blocks[k] == blocks[0], -1.0, cells[k] - 16.0 * blocks[k])
            here = jnp.where(place == at, value, here)
            there = jnp.where(place == past, value, there)
        here, there = here.astype(BF), there.astype(BF)
        following = blocks[0] + 1.0
        following = jnp.where(following >= 32.0, 0.0, following)
        first = jnp.broadcast_to(blocks[0], (16, 128)).astype(BF)
        second = jnp.broadcast_to(following, (16, 128)).astype(BF)
        for part in range(32):
            label = jnp.full((16, 128), part, BF)
            table[16 * part : 16 * part + 16, lane : lane + 128] = jnp.where(
                first == label, here, jnp.where(second == label, there, zero)
            )

    def chunk(n):
        sx_s, wy_s = tables[n % 2]
        for m in range(4):
            fill(4 * n + m, 0, sx_s, 128 * m)
            fill(4 * n + m, 1, wy_s, 128 * m)

    def product(n):
        sx_s, wy_s = tables[n % 2]
        return lax.dot_general(
            sx_s[...], wy_s[...], (((1,), (1,)), ((), ())), preferred_element_type=F32
        )

    chunk(0)
    for n in range(6):
        if n < 5:
            chunk(n + 1)
        if n == 0:
            total_s[...] = product(n)
        elif n < 5:
            total_s[...] += product(n)
    return total_s[...] + product(5)


def spread_kernel(
    p0, p1, p2, p3, p4, p5, p6, p7,
    w1_at, b1_at, w2_at, b2_at, wo_at, bo_at, table_at,
    out_ref, part_ref, h1_ref, t2_ref, to_ref,
    code_s, feat_s, in_s, xin_s, cell_s, wgt_s, sxa_s, wya_s, sxb_s, wyb_s, total_s,
    table_ref, w1_ref, b1_ref, w2_ref, b2_ref, wo_ref, bo_ref, sems,
):
    copies = fetch(
        (
            (w1_at, w1_ref), (b1_at, b1_ref), (w2_at, w2_ref),
            (b2_at, b2_ref), (wo_at, wo_ref), (bo_at, bo_ref),
        ),
        sems,
    )
    (table_copy,) = fetch(((table_at, table_ref),), sems, 6)
    pays = (p0, p1, p2, p3, p4, p5, p6, p7)

    def pay(i, start, stop):
        return pays[i][start:stop, :]

    rim = [
        jnp.concatenate([pay(i, r, r + 1) for i in range(8)], axis=0) for r in (0, 4, 8, 12, 16)
    ]
    for i in range(8):
        code_s[:, i, :] = pay(i, 24, 56)
    for j in range(8):
        turned = [pltpu.roll(v, 16 * j, 1) if j else v for v in rim]
        for s in (-1, 0, 1):
            cand = [pltpu.roll(v, (-s) % 8, 0) if s else v for v in turned]
            dx = wrapped(cand[0] - rim[0]) + (cand[2] - rim[2])
            dy = wrapped(cand[1] - rim[1]) + (cand[3] - rim[3])
            dz = float(s) + (cand[4] - rim[4])
            scale = lax.rsqrt(1.0 + (dx * dx + dy * dy + dz * dz) * (1.0 / 16.0))
            c = (s + 1) * 8 + j
            feat_s[c, 0] = scale
            feat_s[c, 1] = scale * dx * 0.25
            feat_s[c, 2] = scale * dy * 0.25
            feat_s[c, 3] = scale * dz * 0.25

    def choose(block, carry):
        codes = [code_s[block * 4 + m] for m in range(4)]
        held = [[jnp.zeros((8, 128), F32) for _ in range(4)] for _ in range(4)]
        for c in range(24):
            feats = [feat_s[c, f] for f in range(4)]
            for m in range(4):
                mask = codes[m] == float(c)
                for f in range(4):
                    held[m][f] = jnp.where(mask, feats[f], held[m][f])
        for m in range(4):
            for f in range(4):
                in_s[(block * 4 + m) * 4 + f] = held[m][f]
        return carry

    lax.fori_loop(0, 8, choose, 0)
    for i in range(1, 7):
        xin_s[:, (i - 1) * 128 : i * 128] = in_s[:, i, :].astype(BF)
    for copy in copies:
        copy.wait()

    def column(row):
        wide = jnp.concatenate([row, jnp.zeros((1, 256 - row.shape[1]), F32)], axis=1)
        tall = jnp.broadcast_to(wide, (128, 256)).T[0 : row.shape[1]]
        return jnp.concatenate([tall] * 6, axis=1)

    h1 = jnp.tanh(dot(w1_ref[...], xin_s[...]) + column(b1_ref[...]))
    t2 = jnp.tanh(dot_first(w2_ref[...], h1.astype(BF)) + column(b2_ref[...]))
    to = jnp.tanh(dot(wo_ref[...], (t2 + h1).astype(BF)) + column(bo_ref[...]))
    h1_ref[...] = h1[:, 256:640]
    t2_ref[...] = t2[:, 256:640]
    to_ref[...] = to[:, 256:640]
    for n, i in enumerate((3, 4, 5, 2)):
        atom_rows(part_ref, 4 * n, lambda a, b, i=i: pay(i, a, b), float(4 - i))
    for i in range(1, 7):
        row = slice(15 + i, 16 + i)
        lanes = slice((i - 1) * 128, i * 128)
        part_ref[0, row, :] = pay(i, 0, 1)
        part_ref[1, row, :] = pay(i, 4, 5)
        part_ref[2, row, :] = pay(i, 8, 9) + to[0:1, lanes]
        part_ref[3, row, :] = pay(i, 12, 13) + to[1:2, lanes]
        part_ref[4, row, :] = float(4 - i) - (pay(i, 16, 17) + to[2:3, lanes])
        part_ref[5, row, :] = jnp.full((1, 128), CENTROID_CHARGE, F32)
    part_ref[:, 22:24, :] = jnp.zeros((6, 2, 128), F32)
    tables = ((sxa_s, wya_s), (sxb_s, wyb_s))
    density = densities(part_ref, cell_s, wgt_s, tables, total_s)
    table_copy.wait()
    hh, hl = table_ref[0], table_ref[1]
    high, low = split(density)
    inner = dot(high, hh) + dot(low, hh) + dot(high, hl)
    inner = inner.astype(BF)
    spectrum = dot(hh, inner) + dot(hl, inner)
    lower = lax.broadcasted_iota(jnp.int32, (64, 8, 128), 1) < 4
    for g in range(2):
        tile0 = spectrum[:, 256 * g : 256 * g + 128].reshape(64, 8, 128)
        tile1 = spectrum[:, 256 * g + 128 : 256 * g + 256].reshape(64, 8, 128)
        even = jnp.where(lower, tile0, pltpu.roll(tile1, 4, 1))
        odd = jnp.where(lower, pltpu.roll(tile0, 4, 1), tile1)
        out_ref[:, 0, 8 * g : 8 * g + 8, :] = even.astype(BF)
        out_ref[:, 1, 8 * g : 8 * g + 8, :] = odd.astype(BF)


def influence_kernel(group_ref, kept_ref, taken_ref, out_ref):
    mine = pl.multiple_of(group_ref[0] * 128, 128)
    other = pl.multiple_of(128 - mine, 128)
    for r in range(8):
        lanes = slice(128 * r, 128 * r + 128)
        at = pl.multiple_of(2 * mine + 128 * (r // 4), 128)
        out_ref[pl.ds(mine, 128), lanes] = kept_ref[:, r % 4, pl.ds(at, 128)]
        out_ref[pl.ds(other, 128), lanes] = taken_ref[:, r % 4, 128 * (r // 4) : 128 * (r // 4) + 128]


def depth_kernel(
    x_ref, infl_ref, table_at, out_ref, wide_s, xb_s, back_s, table_ref, sems
):
    (table_copy,) = fetch(((table_at, table_ref),), sems)
    wide_s[...] = x_ref[...].astype(F32)
    for r in range(8):
        lanes = slice(128 * r, 128 * r + 128)
        xb_s[0:128, lanes] = wide_s[:, r, :].astype(BF)
        xb_s[128:256, lanes] = wide_s[:, 8 + r, :].astype(BF)
    table_copy.wait()
    fh, fl, ih, il = (table_ref[n] for n in range(4))
    for r in range(0, 8, 2):
        lanes = slice(128 * r, 128 * r + 256)
        xb = xb_s[:, lanes]
        spectrum = dot(fh, xb) + dot(fl, xb)
        high, low = split(spectrum * infl_ref[:, lanes])
        back = dot(ih, high) + dot(il, high) + dot(ih, low)
        for t in range(2):
            column = back[:, 128 * t : 128 * t + 128]
            back_s[:, r + t, :] = column[0:128]
            back_s[:, 8 + r + t, :] = column[128:256]
    out_ref[...] = back_s[...].astype(BF)


def cells_of(part_ref, cell_s, wgt_s, axes):
    for n, axis in enumerate(axes):
        cells, offsets = stencil(part_ref[axis], part_ref[2 + axis])
        for k in range(4):
            cell_s[n * 4 + k] = cells[k]
            wgt_s[n * 8 + k] = spline(offsets[k])
            wgt_s[n * 8 + 4 + k] = spline_slope(offsets[k])


def lookup_kernel(axis, kind, part_ref, out_ref, cell_s, wgt_s):
    cells_of(part_ref, cell_s, wgt_s, (axis,))

    def fill(row, carry):
        row_at = pl.ds(row, 1)
        cells = [cell_s[k, row_at, :] for k in range(4)]
        values = [wgt_s[k, row_at, :] for k in range(4)]
        slopes = [wgt_s[4 + k, row_at, :] for k in range(4)]
        for part in range(16):
            here = lax.broadcasted_iota(jnp.int32, (32, 128), 0).astype(F32) + 32.0 * part
            found = jnp.zeros((32, 128), F32)
            sloped = jnp.zeros((32, 128), F32)
            for k in range(4):
                mask = here == cells[k]
                found = jnp.where(mask, values[k], found)
                sloped = jnp.where(mask, slopes[k], sloped)
            out_ref[row, 32 * part : 32 * part + 32, 0:128] = found.astype(kind)
            out_ref[row, 32 * part : 32 * part + 32, 128:256] = sloped.astype(kind)
        return carry

    lax.fori_loop(0, 22, fill, 0)


def probe_kernel(
    y_ref, part_ref, wx_at, wy_at, table_at,
    pot_at, o0, o1, o2, o3, o4, o5, o6, o7,
    r_s, field_s, va_s, vb_s, push_s, pot_s, wx_ref, wy_ref, table_ref, sems,
):
    outs = (o0, o1, o2, o3, o4, o5, o6, o7)
    half = pl.ds(0, 10), pl.ds(10, 12)
    (table_copy,) = fetch(((table_at, table_ref),), sems, 4)
    copies = fetch(
        (
            (wx_at, wx_ref),
            (wy_at.at[half[0]], wy_ref.at[half[0]]),
            (wy_at.at[half[1]], wy_ref.at[half[1]]),
        ),
        sems,
    )
    lower = lax.broadcasted_iota(jnp.int32, (64, 8, 128), 1) < 4
    for g in range(2):
        even = y_ref[:, 0, 8 * g : 8 * g + 8, :].astype(F32)
        odd = y_ref[:, 1, 8 * g : 8 * g + 8, :].astype(F32)
        tile0 = jnp.where(lower, even, pltpu.roll(odd, 4, 1))
        tile1 = jnp.where(lower, pltpu.roll(even, 4, 1), odd)
        r_s[:, 256 * g : 256 * g + 128] = tile0.reshape(512, 128).astype(BF)
        r_s[:, 256 * g + 128 : 256 * g + 256] = tile1.reshape(512, 128).astype(BF)
    table_copy.wait()
    hh, hl = table_ref[0], table_ref[1]
    inner = dot(hh, r_s[...]) + dot(hl, r_s[...])
    inner = inner.astype(BF)
    potential = (dot(inner, hh) + dot(inner, hl)) * (1.0 / 67108864.0)
    pot_s[...] = potential
    pot_copy = pltpu.make_async_copy(pot_s, pot_at.at[0], sems.at[3])
    pot_copy.start()
    field_s[...] = potential.T.astype(BF)


    def gather(row, vs_s):
        row_at = pl.ds(row, 1)
        probed = jnp.zeros((8, 128), F32)
        along_x = jnp.zeros((8, 128), F32)
        along_y = jnp.zeros((8, 128), F32)
        for part in range(64):
            rows = slice(8 * part, 8 * part + 8)
            found = wy_ref[row, rows, 0:128]
            value = vs_s[rows, 0:128]
            probed = probed + value * found
            along_x = along_x + vs_s[rows, 128:256] * found
            along_y = along_y + value * wy_ref[row, rows, 128:256]
        push_s[0, row_at, :] = jnp.sum(along_x, axis=0, keepdims=True)
        push_s[1, row_at, :] = jnp.sum(along_y, axis=0, keepdims=True)
        push_s[2, row_at, :] = jnp.sum(probed, axis=0, keepdims=True)

    def probe(pair, carry):
        row = 2 * pair
        vb_s[...] = dot(field_s[...], wx_ref[row + 1])
        gather(row, va_s)
        va_s[...] = dot(field_s[...], wx_ref[jnp.minimum(row + 2, 21)])
        gather(row + 1, vb_s)
        return carry

    copies[0].wait()
    va_s[...] = dot(field_s[...], wx_ref[0])
    copies[1].wait()
    lax.fori_loop(0, 5, probe, 0)
    copies[2].wait()
    lax.fori_loop(5, 11, probe, 0)
    pot_copy.wait()
    charge = part_ref[5]
    charge_z = charge * spline(part_ref[4])
    charge_slope = charge * spline_slope(part_ref[4])
    push = [
        push_s[0] * charge_z,
        push_s[1] * charge_z,
        push_s[2] * charge_slope,
    ]
    for i, ref in enumerate(outs):
        ref[...] = jnp.zeros((ROWS, 128), F32)
        for c in range(3):
            if 2 <= i <= 5:
                first = (12, 0, 4, 8)[i - 2]
                ref[4 * c : 4 * c + 4, :] = push[c][first : first + 4]
            for m in range(3):
                source = i - 1 + m
                if 1 <= source <= 6:
                    to = 12 + 3 * c + m
                    ref[to : to + 1, :] = push[c][15 + source : 16 + source]


def force_kernel(
    s0, s1, s2, s3, s4, s5, s6, s7, before_ref, own_ref, after_ref,
    h1_ref, t2_ref, to_ref, w1_ref, w2_ref, wo_ref, out_ref, gin_s,
):
    total = s0[...] + s1[...] + s2[...] + s3[...] + s4[...] + s5[...] + s6[...] + s7[...]
    pull = [
        jnp.concatenate([total[12 + 3 * c + n : 13 + 3 * c + n] for n in range(3)], axis=1)
        for c in range(3)
    ]
    to = to_ref[...]
    g_out = jnp.concatenate(pull, axis=0) * (1.0 - to * to)
    g_two = dot_first(wo_ref[...], g_out.astype(BF))
    t2, h1 = t2_ref[...], h1_ref[...]
    g_pre = g_two * (1.0 - t2 * t2)
    g_one = dot(w2_ref[...], g_pre.astype(BF)) + g_two
    gin_s[...] = dot_first(w1_ref[...], (g_one * (1.0 - h1 * h1)).astype(BF))
    pays = (before_ref, own_ref, after_ref)
    turn = lax.broadcasted_iota(jnp.int32, (8, 128), 0).astype(F32)

    def rims(ref):
        return [ref[r : r + 1, :] for r in (0, 4, 8, 12, 16)]

    def rolled(row):
        return jnp.concatenate([pltpu.roll(row, 16 * j, 1) if j else row for j in range(8)], axis=0)

    own_rim = rims(own_ref)
    turned = [[rolled(row) for row in rims(ref)] for ref in pays]
    force = [total[4 * c : 4 * c + 1] for c in range(3)]
    owner_sum = [jnp.zeros((8, 128), F32) for _ in range(3)]
    for n, s in ((0, 1), (1, -1), (1, 0), (1, 1), (2, -1)):
        owner = rims(pays[n])
        cand = turned[n + s]
        dx = wrapped(cand[0] - owner[0]) + (cand[2] - owner[2])
        dy = wrapped(cand[1] - owner[1]) + (cand[3] - owner[3])
        dz = float(s) + (cand[4] - owner[4])
        scale = lax.rsqrt(1.0 + (dx * dx + dy * dy + dz * dz) * (1.0 / 16.0))
        lanes = slice(128 * n, 128 * n + 128)
        mine = turn + float(8 * (s + 1))
        cots = [jnp.zeros((8, 128), F32) for _ in range(4)]
        for m in range(NEIGH):
            mask = pays[n][24 + m : 25 + m, :] == mine
            for f in range(4):
                cots[f] = cots[f] + jnp.where(mask, gin_s[4 * m + f : 4 * m + f + 1, lanes], 0.0)
        along = cots[0] + (cots[1] * dx + cots[2] * dy + cots[3] * dz) * 0.25
        common = along * (scale * scale * scale) * (-1.0 / 16.0)
        moved = [
            common * dx + cots[1] * scale * 0.25,
            common * dy + cots[2] * scale * 0.25,
            common * dz + cots[3] * scale * 0.25,
        ]
        if n == 1:
            owner_sum = [owner_sum[c] + moved[c] for c in range(3)]
        if n + s == 1:
            for c in range(3):
                for j in range(8):
                    row = moved[c][j : j + 1]
                    force[c] = force[c] + (pltpu.roll(row, (-16 * j) % 128, 1) if j else row)
    for c in range(3):
        own = force[c] + pull[c][:, 128:256] - jnp.sum(owner_sum[c], axis=0, keepdims=True)
        out_ref[c : c + 1, 0:128] = own
        for k in range(1, 4):
            out_ref[c : c + 1, 128 * k : 128 * k + 128] = total[4 * c + k : 4 * c + k + 1]


VM = pl.BlockSpec(memory_space=pltpu.VMEM)


SM = pl.BlockSpec(memory_space=pltpu.SMEM)
HB = pl.BlockSpec(memory_space=pltpu.HBM)


def call(kernel, inputs, outs, scratch=(), limit=16, spaces=None, first=None, flops=0):
    spaces = spaces or {}
    out_specs = jax.tree.map(lambda _: VM, outs)
    if first is not None:
        out_specs = (first,) + tuple(out_specs)[1:]
    return pl.pallas_call(
        kernel,
        out_shape=outs,
        in_specs=[spaces.get(n, VM) for n in range(len(inputs))],
        out_specs=out_specs,
        scratch_shapes=list(scratch),
        compiler_params=pltpu.CompilerParams(vmem_limit_bytes=limit * MIB),
        cost_estimate=pl.CostEstimate(flops=flops, bytes_accessed=4 * MIB, transcendentals=0),
    )(*inputs)


def shape(*dims, dtype=F32):
    return jax.ShapeDtypeStruct(dims, dtype)


def body(
    base_index,
    fraction,
    charge,
    atom_count,
    owner_index,
    neighbour,
    influence,
    layer_one,
    bias_one,
    layer_two,
    bias_two,
    layer_out,
    bias_out,
):
    both = ("slab", "grp")
    devices = 256
    group = lax.axis_index("grp")

    def from_device(value, step):
        pairs = [(source, (source - step) % devices) for source in range(devices)]
        return lax.ppermute(value, both, pairs)

    planes = jnp.asarray(np.stack(cas_pair(np.arange(NX), np.arange(NX), NX)))
    split_z = np.concatenate([np.arange(0, NZ, 2), np.arange(1, NZ, 2)])
    fore = cas_pair(np.arange(NZ), split_z, NZ)
    back = cas_pair(split_z, np.arange(NZ), NZ)

    with jax.named_scope("pack"):
        payload = call(
            pack_kernel,
            (
                atom_count,
                base_index,
                fraction,
                charge.reshape(4, 128),
                owner_index.reshape(1, 128),
                neighbour,
            ),
            shape(56, 128),
            (
                pltpu.VMEM((3, 512), jnp.int32),
                pltpu.VMEM((3, 512), F32),
                pltpu.VMEM((4, 128), F32),
                pltpu.VMEM((1, 128), jnp.int32),
                pltpu.VMEM((NEIGH, 128), jnp.int32),
                pltpu.SemaphoreType.DMA((5,)),
            ),
            spaces={0: SM, 1: HB, 2: HB, 3: HB, 4: HB, 5: HB},
            limit=59,
        )
    with jax.named_scope("particles_in"):
        pays = [payload if step == 0 else from_device(payload, step) for step in NEAR]
    where = group.astype(jnp.int32).reshape(1)
    with jax.named_scope("influence_swap"):
        given = lax.dynamic_slice_in_dim(influence, (1 - group) * 256, 256, axis=2).astype(BF)
        given, *pays = lax.optimization_barrier((given, *pays))
        taken = lax.ppermute(given, "grp", [(0, 1), (1, 0)])
    with jax.named_scope("spread"):
        columns, part, h1, t2, to = call(
            spread_kernel,
            (
                *pays,
                layer_one.T,
                bias_one.reshape(1, -1),
                layer_two,
                bias_two.reshape(1, -1),
                layer_out.T,
                bias_out.reshape(1, -1),
                planes,
            ),
            (
                shape(64, 2, 16, 128, dtype=BF),
                shape(6, ROWS, 128),
                shape(HID, 384),
                shape(HID, 384),
                shape(3, 384),
            ),
            (
                pltpu.VMEM((NEIGH, 8, 128), F32),
                pltpu.VMEM((24, 4, 8, 128), F32),
                pltpu.VMEM((128, 8, 128), F32),
                pltpu.VMEM((128, 768), BF),
                pltpu.VMEM((8, ROWS, 128), F32),
                pltpu.VMEM((8, ROWS, 128), F32),
                pltpu.VMEM((NX, 512), BF),
                pltpu.VMEM((NY, 512), BF),
                pltpu.VMEM((NX, 512), BF),
                pltpu.VMEM((NY, 512), BF),
                pltpu.VMEM((NX, NY), F32),
                pltpu.VMEM((2, NX, NX), BF),
                pltpu.VMEM((HID, 128), BF),
                pltpu.VMEM((1, HID), F32),
                pltpu.VMEM((HID, HID), BF),
                pltpu.VMEM((1, HID), F32),
                pltpu.VMEM((3, HID), BF),
                pltpu.VMEM((1, 3), F32),
                pltpu.SemaphoreType.DMA((7,)),
            ),
            limit=58,
            spaces={n: HB for n in range(8, 15)},
            flops=4_000_000_000,
        )
    columns, taken = lax.optimization_barrier((columns, taken))
    with jax.named_scope("to_columns"):
        columns = lax.all_to_all(columns.reshape(256, 8, 128), both, 0, 0, tiled=True)
    def lookup(axis, kind):
        return call(
            lambda *refs: lookup_kernel(axis, kind, *refs),
            (part,),
            shape(22, NX, 256, dtype=kind),
            (pltpu.VMEM((4, ROWS, 128), F32), pltpu.VMEM((8, ROWS, 128), F32)),
            limit=58,
            flops=4_000_000_000,
        )

    with jax.named_scope("lookup_x"):
        weights_x = lookup(0, BF)
    with jax.named_scope("influence"):
        infl = call(
            influence_kernel,
            (where, influence, taken.astype(F32)),
            shape(NZ, 1024),
            spaces={0: SM},
        )
    with jax.named_scope("depth"):
        rows = call(
            depth_kernel,
            (
                columns.reshape(128, 16, 128),
                infl,
                jnp.asarray(np.stack(fore + back)),
            ),
            shape(128, 16, 128, dtype=BF),
            (
                pltpu.VMEM((128, 16, 128), F32),
                pltpu.VMEM((NZ, 1024), BF),
                pltpu.VMEM((128, 16, 128), F32),
                pltpu.VMEM((4, NZ, NZ), BF),
                pltpu.SemaphoreType.DMA((1,)),
            ),
            spaces={2: HB},
            limit=50,
            flops=800_000_000,
        )
    with jax.named_scope("to_planes"):
        rows = lax.all_to_all(rows.reshape(256, 8, 128), both, 0, 0, tiled=True)
    with jax.named_scope("lookup_y"):
        weights_y = lookup(1, F32)
    with jax.named_scope("probe"):
        potential, *pushes = call(
            probe_kernel,
            (rows.reshape(64, 2, 16, 128), part, weights_x, weights_y, planes),
            (shape(1, NX, NY),) + (shape(ROWS, 128),) * 8,
            (
                pltpu.VMEM((NX, NY), BF),
                pltpu.VMEM((NY, NX), BF),
                pltpu.VMEM((NY, 256), F32),
                pltpu.VMEM((NY, 256), F32),
                pltpu.VMEM((3, ROWS, 128), F32),
                pltpu.VMEM((NX, NY), F32),
                pltpu.VMEM((22, NX, 256), BF),
                pltpu.VMEM((22, NY, 256), F32),
                pltpu.VMEM((2, NX, NX), BF),
                pltpu.SemaphoreType.DMA((5,)),
            ),
            first=HB,
            limit=52,
            spaces={2: HB, 3: HB, 4: HB},
            flops=5_000_000_000,
        )
    with jax.named_scope("pushes_out"):
        sums = [
            push if step == 0 else from_device(push, -step) for step, push in zip(NEAR, pushes)
        ]
    with jax.named_scope("force"):
        force = call(
            force_kernel,
            (*sums, pays[3], payload, pays[5], h1, t2, to, layer_one.T, layer_two, layer_out.T),
            shape(3, 512),
            (pltpu.VMEM((128, 384), F32),),
            limit=16,
        )
    return force, potential


def solution(mesh):
    return jax.shard_map(
        body,
        mesh=mesh,
        in_specs=(
            P(None, ("slab", "grp")),
            P(None, ("slab", "grp")),
            P(("slab", "grp")),
            P(("slab", "grp")),
            P(("slab", "grp")),
            P(None, ("slab", "grp")),
            P("grp", "slab", None),
            P(),
            P(),
            P(),
            P(),
            P(),
            P(),
        ),
        out_specs=(P(None, ("slab", "grp")), P(("slab", "grp"), None, None)),
        check_vma=False,
    )
```

```python
import functools

import jax
import jax.numpy as jnp
import ml_dtypes
import numpy as np
from jax import lax
from jax.experimental import pallas as pl
from jax.experimental.pallas import tpu as pltpu
from jax.sharding import Mesh
from jax.sharding import PartitionSpec as P

NX = 512
NY = 512
NZ = 256
NEIGH = 32
HID = 240
CENTROID_CHARGE = -2.0
BF = jnp.bfloat16
F32 = jnp.float32
ROWS = 24
NEAR = tuple(range(-4, 4))
MIB = 1024 * 1024


def cas_pair(row_ids, column_ids, period):
    angle = 2.0 * np.pi / period * (np.outer(row_ids, column_ids) % period)
    table = np.cos(angle) + np.sin(angle)
    high = table.astype(ml_dtypes.bfloat16)
    low = (table - high.astype(np.float64)).astype(ml_dtypes.bfloat16)
    return high, low


def spline(offset):
    size = jnp.abs(offset)
    inner = 2.0 / 3.0 - size * size + 0.5 * size * size * size
    rest = 2.0 - size
    outer = rest * rest * rest * (1.0 / 6.0)
    return jnp.where(size < 1.0, inner, jnp.where(size < 2.0, outer, 0.0))


def spline_slope(offset):
    size = jnp.abs(offset)
    sign = jnp.where(offset > 0.0, 1.0, jnp.where(offset < 0.0, -1.0, 0.0))
    inner = (-2.0 * size + 1.5 * size * size) * sign
    rest = 2.0 - size
    outer = -0.5 * rest * rest * sign
    return jnp.where(size < 1.0, inner, jnp.where(size < 2.0, outer, 0.0))


def wrapped(values):
    return jnp.where(
        values >= 256.0, values - 512.0, jnp.where(values < -256.0, values + 512.0, values)
    )


def dot(left, right):
    return jnp.dot(left, right, preferred_element_type=F32)


def dot_first(left, right):
    return lax.dot_general(left, right, (((0,), (0,)), ((), ())), preferred_element_type=F32)


def split(values):
    high = values.astype(BF)
    low = (values - high.astype(F32)).astype(BF)
    return high, low


def chip_of(device):
    device = device % 256
    place = device % 8
    return device // 8 * 4 + place // 4 * 2 + place % 2, place // 2 % 2


def device_of(chip, core):
    chip = chip % 128
    return chip // 4 * 8 + chip % 4 // 2 * 4 + core * 2 + chip % 2


def chip_steps(kind):
    pairs = []
    for chip in range(128):
        if kind < 2:
            pairs.append((device_of(chip - kind - 1, 0), device_of(chip, 0)))
            pairs.append((device_of(chip + kind + 1, 1), device_of(chip, 1)))
        else:
            other = chip - 3 if chip % 2 else chip + 3
            pairs.append((device_of(other, 0), device_of(chip, 0)))
    return pairs


def row_index(place, step):
    there = place + step
    inner = there & 7
    chip = (there >> 3) * 4 + ((inner >> 2) & 1) * 2 + (inner & 1)
    away = chip - (((place >> 2) & 1) * 2 + (place & 1))
    first = jnp.where(away == 1, 6, jnp.where(away == 2, 8, 4))
    first = jnp.where(away == -1, 0, jnp.where(away == -2, 2, first))
    return jnp.where(away == 0, 12, first) + ((inner >> 1) & 1)


def fetch(pairs, sems, first=0):
    copies = [
        pltpu.make_async_copy(source, target, sems.at[first + n])
        for n, (source, target) in enumerate(pairs)
    ]
    for copy in copies:
        copy.start()
    return copies


def pack_kernel(
    count_ref, base_at, frac_at, charge_at, owner_at, near_at,
    out_ref, base_ref, frac_ref, charge_ref, owner_ref, near_ref, sems,
):
    arrays = (
        (base_at, base_ref), (frac_at, frac_ref), (charge_at, charge_ref),
        (owner_at, owner_ref), (near_at, near_ref),
    )
    copies = [pltpu.make_async_copy(a, b, sems.at[n]) for n, (a, b) in enumerate(arrays)]
    for copy in copies:
        copy.start()
    for copy in copies:
        copy.wait()
    for k in range(4):
        lanes = slice(128 * k, 128 * (k + 1))
        out_ref[k : k + 1, :] = base_ref[0:1, lanes].astype(F32)
        out_ref[4 + k : 5 + k, :] = base_ref[1:2, lanes].astype(F32)
        for c in range(3):
            out_ref[8 + 4 * c + k : 9 + 4 * c + k, :] = frac_ref[c : c + 1, lanes]
        slot = lax.broadcasted_iota(jnp.int32, (1, 128), 1) + 128 * k
        out_ref[20 + k : 21 + k, :] = jnp.where(
            slot < count_ref[0], charge_ref[k : k + 1, :], 0.0
        )
    owner = owner_ref[...]
    near = near_ref[...]
    side = jnp.where(near < 128, 0, jnp.where(near < 256, 8, 16))
    code = side + (((owner >> 4) - ((near & 127) >> 4)) & 7)
    atom = lax.broadcasted_iota(jnp.int32, (128, 128), 0)
    chosen = jnp.where(atom == owner, 1.0, 0.0).astype(BF)
    out_ref[24:56, :] = lax.dot_general(
        code.astype(F32).astype(BF), chosen, (((1,), (1,)), ((), ())), preferred_element_type=F32
    )


def atom_rows(part_ref, first, pay, plane):
    rows = slice(first, first + 4)
    for c in range(4):
        part_ref[c, rows, :] = pay(4 * c, 4 * c + 4)
    part_ref[4, rows, :] = plane - pay(16, 20)
    part_ref[5, rows, :] = pay(20, 24)


def stencil(base, frac):
    whole = jnp.floor(frac)
    cells, offsets = [], []
    for k in range(4):
        step = whole + float(k - 1)
        cell = base + step
        cell = jnp.where(cell < 0.0, cell + 512.0, jnp.where(cell >= 512.0, cell - 512.0, cell))
        cells.append(cell)
        offsets.append(step - frac)
    return cells, offsets


def densities(part_ref, cell_s, wgt_s, tables, total_s):
    charge_z = part_ref[5] * spline(part_ref[4])
    for axis in range(2):
        cells, offsets = stencil(part_ref[axis], part_ref[2 + axis])
        for k in range(4):
            value = spline(offsets[k])
            cell_s[axis * 4 + k] = cells[k]
            wgt_s[axis * 4 + k] = charge_z * value if axis == 0 else value
    place = lax.broadcasted_iota(jnp.int32, (16, 128), 0).astype(F32)
    zero = jnp.zeros((16, 128), BF)

    def fill(row, axis, table, lane):
        cells = [cell_s[axis * 4 + k, row : row + 1, :] for k in range(4)]
        blocks = [jnp.floor(cell * (1.0 / 16.0)) for cell in cells]
        here, there = jnp.zeros((16, 128), F32), jnp.zeros((16, 128), F32)
        for k in range(4):
            value = wgt_s[axis * 4 + k, row : row + 1, :]
            at = jnp.where(blocks[k] == blocks[0], cells[k] - 16.0 * blocks[k], -1.0)
            past = jnp.where(blocks[k] == blocks[0], -1.0, cells[k] - 16.0 * blocks[k])
            here = jnp.where(place == at, value, here)
            there = jnp.where(place == past, value, there)
        here, there = here.astype(BF), there.astype(BF)
        following = blocks[0] + 1.0
        following = jnp.where(following >= 32.0, 0.0, following)
        first = jnp.broadcast_to(blocks[0], (16, 128)).astype(BF)
        second = jnp.broadcast_to(following, (16, 128)).astype(BF)
        for part in range(32):
            label = jnp.full((16, 128), part, BF)
            table[16 * part : 16 * part + 16, lane : lane + 128] = jnp.where(
                first == label, here, jnp.where(second == label, there, zero)
            )

    def chunk(n):
        sx_s, wy_s = tables[n % 2]
        for m in range(4):
            fill(4 * n + m, 0, sx_s, 128 * m)
            fill(4 * n + m, 1, wy_s, 128 * m)

    def product(n):
        sx_s, wy_s = tables[n % 2]
        return lax.dot_general(
            sx_s[...], wy_s[...], (((1,), (1,)), ((), ())), preferred_element_type=F32
        )

    chunk(0)
    for n in range(6):
        if n < 5:
            chunk(n + 1)
        if n == 0:
            total_s[...] = product(n)
        elif n < 5:
            total_s[...] += product(n)
    return total_s[...] + product(5)


def spread_kernel(
    place_ref, far_ref, pair_ref,
    w1_at, b1_at, w2_at, b2_at, wo_at, bo_at, table_at, infl_at,
    out_ref, part_ref, h1_ref, t2_ref, to_ref, beside_ref, given_ref,
    rows_s, code_s, feat_s, in_s, xin_s, cell_s, wgt_s, sxa_s, wya_s, sxb_s, wyb_s, total_s,
    table_ref, w1_ref, b1_ref, w2_ref, b2_ref, wo_ref, bo_ref, half_s, sems,
):
    copies = fetch(
        (
            (w1_at, w1_ref), (b1_at, b1_ref), (w2_at, w2_ref),
            (b2_at, b2_ref), (wo_at, wo_ref), (bo_at, bo_ref),
        ),
        sems,
    )
    away = pl.multiple_of(256 - (place_ref[0] & 1) * 256, 256)
    table_copy, half_copy = fetch(
        ((table_at, table_ref), (infl_at.at[:, :, pl.ds(away, 256)], half_s)), sems, 6
    )
    index = [row_index(place_ref[0], step) for step in NEAR]
    rows_s[0:12] = far_ref[...]
    rows_s[12:14] = pair_ref[...]

    def pay(i, start, stop):
        return rows_s[index[i], start:stop, :]

    beside_ref[0] = pay(3, 0, 56)
    beside_ref[1] = pay(5, 0, 56)

    rim = [
        jnp.concatenate([pay(i, r, r + 1) for i in range(8)], axis=0) for r in (0, 4, 8, 12, 16)
    ]
    for i in range(8):
        code_s[:, i, :] = pay(i, 24, 56)
    for j in range(8):
        turned = [pltpu.roll(v, 16 * j, 1) if j else v for v in rim]
        for s in (-1, 0, 1):
            cand = [pltpu.roll(v, (-s) % 8, 0) if s else v for v in turned]
            dx = wrapped(cand[0] - rim[0]) + (cand[2] - rim[2])
            dy = wrapped(cand[1] - rim[1]) + (cand[3] - rim[3])
            dz = float(s) + (cand[4] - rim[4])
            scale = lax.rsqrt(1.0 + (dx * dx + dy * dy + dz * dz) * (1.0 / 16.0))
            c = (s + 1) * 8 + j
            feat_s[c, 0] = scale
            feat_s[c, 1] = scale * dx * 0.25
            feat_s[c, 2] = scale * dy * 0.25
            feat_s[c, 3] = scale * dz * 0.25

    def choose(block, carry):
        codes = [code_s[block * 4 + m] for m in range(4)]
        held = [[jnp.zeros((8, 128), F32) for _ in range(4)] for _ in range(4)]
        for c in range(24):
            feats = [feat_s[c, f] for f in range(4)]
            for m in range(4):
                mask = codes[m] == float(c)
                for f in range(4):
                    held[m][f] = jnp.where(mask, feats[f], held[m][f])
        for m in range(4):
            for f in range(4):
                in_s[(block * 4 + m) * 4 + f] = held[m][f]
        return carry

    lax.fori_loop(0, 8, choose, 0)
    for i in range(1, 7):
        xin_s[:, (i - 1) * 128 : i * 128] = in_s[:, i, :].astype(BF)
    for copy in copies:
        copy.wait()

    def column(row):
        wide = jnp.concatenate([row, jnp.zeros((1, 256 - row.shape[1]), F32)], axis=1)
        tall = jnp.broadcast_to(wide, (128, 256)).T[0 : row.shape[1]]
        return jnp.concatenate([tall] * 6, axis=1)

    h1 = jnp.tanh(dot(w1_ref[...], xin_s[...]) + column(b1_ref[...]))
    t2 = jnp.tanh(dot_first(w2_ref[...], h1.astype(BF)) + column(b2_ref[...]))
    to = jnp.tanh(dot(wo_ref[...], (t2 + h1).astype(BF)) + column(bo_ref[...]))
    h1_ref[...] = h1[:, 256:640]
    t2_ref[...] = t2[:, 256:640]
    to_ref[...] = to[:, 256:640]
    for n, i in enumerate((3, 4, 5, 2)):
        atom_rows(part_ref, 4 * n, lambda a, b, i=i: pay(i, a, b), float(4 - i))
    for i in range(1, 7):
        row = slice(15 + i, 16 + i)
        lanes = slice((i - 1) * 128, i * 128)
        part_ref[0, row, :] = pay(i, 0, 1)
        part_ref[1, row, :] = pay(i, 4, 5)
        part_ref[2, row, :] = pay(i, 8, 9) + to[0:1, lanes]
        part_ref[3, row, :] = pay(i, 12, 13) + to[1:2, lanes]
        part_ref[4, row, :] = float(4 - i) - (pay(i, 16, 17) + to[2:3, lanes])
        part_ref[5, row, :] = jnp.full((1, 128), CENTROID_CHARGE, F32)
    part_ref[:, 22:24, :] = jnp.zeros((6, 2, 128), F32)
    tables = ((sxa_s, wya_s), (sxb_s, wyb_s))
    density = densities(part_ref, cell_s, wgt_s, tables, total_s)
    half_copy.wait()
    given_ref[...] = half_s[...].astype(BF)
    table_copy.wait()
    hh = table_ref[...]
    high, low = split(density)
    inner = (dot(high, hh) + dot(low, hh)).astype(BF)
    spectrum = dot(hh, inner)
    lower = lax.broadcasted_iota(jnp.int32, (64, 8, 128), 1) < 4
    for g in range(2):
        tile0 = spectrum[:, 256 * g : 256 * g + 128].reshape(64, 8, 128)
        tile1 = spectrum[:, 256 * g + 128 : 256 * g + 256].reshape(64, 8, 128)
        even = jnp.where(lower, tile0, pltpu.roll(tile1, 4, 1))
        odd = jnp.where(lower, pltpu.roll(tile0, 4, 1), tile1)
        out_ref[:, 0, 8 * g : 8 * g + 8, :] = even.astype(BF)
        out_ref[:, 1, 8 * g : 8 * g + 8, :] = odd.astype(BF)


def influence_kernel(group_ref, kept_ref, taken_ref, out_ref):
    mine = pl.multiple_of((group_ref[0] & 1) * 128, 128)
    other = pl.multiple_of(128 - mine, 128)
    for r in range(8):
        lanes = slice(128 * r, 128 * r + 128)
        at = pl.multiple_of(2 * mine + 128 * (r // 4), 128)
        out_ref[pl.ds(mine, 128), lanes] = kept_ref[:, r % 4, pl.ds(at, 128)]
        out_ref[pl.ds(other, 128), lanes] = taken_ref[:, r % 4, 128 * (r // 4) : 128 * (r // 4) + 128]


def depth_kernel(
    x_ref, infl_ref, table_ref, out_ref, wide_s, xb_s, back_s
):
    wide_s[...] = x_ref[...].astype(F32)
    for r in range(8):
        lanes = slice(128 * r, 128 * r + 128)
        xb_s[0:128, lanes] = wide_s[:, r, :].astype(BF)
        xb_s[128:256, lanes] = wide_s[:, 8 + r, :].astype(BF)
    fh, fl, ih, il = (table_ref[n] for n in range(4))
    for r in range(0, 8, 2):
        lanes = slice(128 * r, 128 * r + 256)
        xb = xb_s[:, lanes]
        spectrum = dot(fh, xb) + dot(fl, xb)
        weighted = (spectrum * infl_ref[:, lanes]).astype(BF)
        back = dot(ih, weighted) + dot(il, weighted)
        for t in range(2):
            column = back[:, 128 * t : 128 * t + 128]
            back_s[:, r + t, :] = column[0:128]
            back_s[:, 8 + r + t, :] = column[128:256]
    out_ref[...] = back_s[...].astype(BF)


def cells_of(part_ref, cell_s, wgt_s, axes):
    for n, axis in enumerate(axes):
        cells, offsets = stencil(part_ref[axis], part_ref[2 + axis])
        for k in range(4):
            cell_s[n * 4 + k] = cells[k]
            wgt_s[n * 8 + k] = spline(offsets[k])
            wgt_s[n * 8 + 4 + k] = spline_slope(offsets[k])


def lookup_kernel(axis, kind, part_ref, out_ref, cell_s, wgt_s):
    cells_of(part_ref, cell_s, wgt_s, (axis,))

    def fill(row, carry):
        row_at = pl.ds(row, 1)
        cells = [cell_s[k, row_at, :] for k in range(4)]
        values = [wgt_s[k, row_at, :] for k in range(4)]
        slopes = [wgt_s[4 + k, row_at, :] for k in range(4)]
        for part in range(16):
            here = lax.broadcasted_iota(jnp.int32, (32, 128), 0).astype(F32) + 32.0 * part
            found = jnp.zeros((32, 128), F32)
            sloped = jnp.zeros((32, 128), F32)
            for k in range(4):
                mask = here == cells[k]
                found = jnp.where(mask, values[k], found)
                sloped = jnp.where(mask, slopes[k], sloped)
            out_ref[row, 32 * part : 32 * part + 32, 0:128] = found.astype(kind)
            out_ref[row, 32 * part : 32 * part + 32, 128:256] = sloped.astype(kind)
        return carry

    lax.fori_loop(0, 22, fill, 0)


def probe_kernel(
    y_ref, part_ref, wx_at, wy_at, table_at,
    pot_at, o0, o1, o2, o3, o4, o5, o6, o7,
    r_s, field_s, va_s, vb_s, push_s, pot_s, wx_ref, wy_ref, table_ref, sems,
):
    outs = (o0, o1, o2, o3, o4, o5, o6, o7)
    half = pl.ds(0, 10), pl.ds(10, 12)
    (table_copy,) = fetch(((table_at, table_ref),), sems, 4)
    copies = fetch(
        (
            (wx_at, wx_ref),
            (wy_at.at[half[0]], wy_ref.at[half[0]]),
            (wy_at.at[half[1]], wy_ref.at[half[1]]),
        ),
        sems,
    )
    lower = lax.broadcasted_iota(jnp.int32, (64, 8, 128), 1) < 4
    for g in range(2):
        even = y_ref[:, 0, 8 * g : 8 * g + 8, :].astype(F32)
        odd = y_ref[:, 1, 8 * g : 8 * g + 8, :].astype(F32)
        tile0 = jnp.where(lower, even, pltpu.roll(odd, 4, 1))
        tile1 = jnp.where(lower, pltpu.roll(even, 4, 1), odd)
        r_s[:, 256 * g : 256 * g + 128] = tile0.reshape(512, 128).astype(BF)
        r_s[:, 256 * g + 128 : 256 * g + 256] = tile1.reshape(512, 128).astype(BF)
    table_copy.wait()
    hh = table_ref[...]
    inner = dot(hh, r_s[...])
    inner = inner.astype(BF)
    potential = dot(inner, hh) * (1.0 / 67108864.0)
    pot_s[...] = potential
    pot_copy = pltpu.make_async_copy(pot_s, pot_at.at[0], sems.at[3])
    pot_copy.start()
    field_s[...] = potential.T.astype(BF)


    def gather(row, vs_s):
        row_at = pl.ds(row, 1)
        probed = jnp.zeros((8, 128), F32)
        along_x = jnp.zeros((8, 128), F32)
        along_y = jnp.zeros((8, 128), F32)
        for part in range(64):
            rows = slice(8 * part, 8 * part + 8)
            found = wy_ref[row, rows, 0:128]
            value = vs_s[rows, 0:128]
            probed = probed + value * found
            along_x = along_x + vs_s[rows, 128:256] * found
            along_y = along_y + value * wy_ref[row, rows, 128:256]
        push_s[0, row_at, :] = jnp.sum(along_x, axis=0, keepdims=True)
        push_s[1, row_at, :] = jnp.sum(along_y, axis=0, keepdims=True)
        push_s[2, row_at, :] = jnp.sum(probed, axis=0, keepdims=True)

    def probe(pair, carry):
        row = 2 * pair
        vb_s[...] = dot(field_s[...], wx_ref[row + 1])
        gather(row, va_s)
        va_s[...] = dot(field_s[...], wx_ref[jnp.minimum(row + 2, 21)])
        gather(row + 1, vb_s)
        return carry

    copies[0].wait()
    va_s[...] = dot(field_s[...], wx_ref[0])
    copies[1].wait()
    lax.fori_loop(0, 5, probe, 0)
    copies[2].wait()
    lax.fori_loop(5, 11, probe, 0)
    pot_copy.wait()
    charge = part_ref[5]
    charge_z = charge * spline(part_ref[4])
    charge_slope = charge * spline_slope(part_ref[4])
    push = [
        push_s[0] * charge_z,
        push_s[1] * charge_z,
        push_s[2] * charge_slope,
    ]
    for i, ref in enumerate(outs):
        ref[...] = jnp.zeros((ROWS, 128), F32)
        for c in range(3):
            if 2 <= i <= 5:
                first = (12, 0, 4, 8)[i - 2]
                ref[4 * c : 4 * c + 4, :] = push[c][first : first + 4]
            for m in range(3):
                source = i - 1 + m
                if 1 <= source <= 6:
                    to = 12 + 3 * c + m
                    ref[to : to + 1, :] = push[c][15 + source : 16 + source]


def force_kernel(
    s0, s1, s2, s3, s4, s5, s6, s7, beside_ref, own_ref,
    h1_ref, t2_ref, to_ref, w1_ref, w2_ref, wo_ref, out_ref, gin_s,
):
    total = s0[...] + s1[...] + s2[...] + s3[...] + s4[...] + s5[...] + s6[...] + s7[...]
    pull = [
        jnp.concatenate([total[12 + 3 * c + n : 13 + 3 * c + n] for n in range(3)], axis=1)
        for c in range(3)
    ]
    to = to_ref[...]
    g_out = jnp.concatenate(pull, axis=0) * (1.0 - to * to)
    g_two = dot_first(wo_ref[...], g_out.astype(BF))
    t2, h1 = t2_ref[...], h1_ref[...]
    g_pre = g_two * (1.0 - t2 * t2)
    g_one = dot(w2_ref[...], g_pre.astype(BF)) + g_two
    gin_s[...] = dot_first(w1_ref[...], (g_one * (1.0 - h1 * h1)).astype(BF))
    pays = (beside_ref.at[0], own_ref, beside_ref.at[1])
    turn = lax.broadcasted_iota(jnp.int32, (8, 128), 0).astype(F32)

    def rims(ref):
        return [ref[r : r + 1, :] for r in (0, 4, 8, 12, 16)]

    def rolled(row):
        return jnp.concatenate([pltpu.roll(row, 16 * j, 1) if j else row for j in range(8)], axis=0)

    own_rim = rims(own_ref)
    turned = [[rolled(row) for row in rims(ref)] for ref in pays]
    force = [total[4 * c : 4 * c + 1] for c in range(3)]
    owner_sum = [jnp.zeros((8, 128), F32) for _ in range(3)]
    for n, s in ((0, 1), (1, -1), (1, 0), (1, 1), (2, -1)):
        owner = rims(pays[n])
        cand = turned[n + s]
        dx = wrapped(cand[0] - owner[0]) + (cand[2] - owner[2])
        dy = wrapped(cand[1] - owner[1]) + (cand[3] - owner[3])
        dz = float(s) + (cand[4] - owner[4])
        scale = lax.rsqrt(1.0 + (dx * dx + dy * dy + dz * dz) * (1.0 / 16.0))
        lanes = slice(128 * n, 128 * n + 128)
        mine = turn + float(8 * (s + 1))
        cots = [jnp.zeros((8, 128), F32) for _ in range(4)]
        for m in range(NEIGH):
            mask = pays[n][24 + m : 25 + m, :] == mine
            for f in range(4):
                cots[f] = cots[f] + jnp.where(mask, gin_s[4 * m + f : 4 * m + f + 1, lanes], 0.0)
        along = cots[0] + (cots[1] * dx + cots[2] * dy + cots[3] * dz) * 0.25
        common = along * (scale * scale * scale) * (-1.0 / 16.0)
        moved = [
            common * dx + cots[1] * scale * 0.25,
            common * dy + cots[2] * scale * 0.25,
            common * dz + cots[3] * scale * 0.25,
        ]
        if n == 1:
            owner_sum = [owner_sum[c] + moved[c] for c in range(3)]
        if n + s == 1:
            for c in range(3):
                for j in range(8):
                    row = moved[c][j : j + 1]
                    force[c] = force[c] + (pltpu.roll(row, (-16 * j) % 128, 1) if j else row)
    for c in range(3):
        own = force[c] + pull[c][:, 128:256] - jnp.sum(owner_sum[c], axis=0, keepdims=True)
        out_ref[c : c + 1, 0:128] = own
        for k in range(1, 4):
            out_ref[c : c + 1, 128 * k : 128 * k + 128] = total[4 * c + k : 4 * c + k + 1]


VM = pl.BlockSpec(memory_space=pltpu.VMEM)


SM = pl.BlockSpec(memory_space=pltpu.SMEM)
HB = pl.BlockSpec(memory_space=pltpu.HBM)


def call(kernel, inputs, outs, scratch=(), limit=16, spaces=None, first=None, flops=0):
    spaces = spaces or {}
    out_specs = jax.tree.map(lambda _: VM, outs)
    if first is not None:
        out_specs = (first,) + tuple(out_specs)[1:]
    return pl.pallas_call(
        kernel,
        out_shape=outs,
        in_specs=[spaces.get(n, VM) for n in range(len(inputs))],
        out_specs=out_specs,
        scratch_shapes=list(scratch),
        compiler_params=pltpu.CompilerParams(vmem_limit_bytes=limit * MIB),
        cost_estimate=pl.CostEstimate(flops=flops, bytes_accessed=4 * MIB, transcendentals=0),
    )(*inputs)


def shape(*dims, dtype=F32):
    return jax.ShapeDtypeStruct(dims, dtype)


def body(
    base_index,
    fraction,
    charge,
    atom_count,
    owner_index,
    neighbour,
    influence,
    layer_one,
    bias_one,
    layer_two,
    bias_two,
    layer_out,
    bias_out,
):
    both = ("row", "core", "grp")
    devices = 256

    def from_device(value, step):
        pairs = [(source, (source - step) % devices) for source in range(devices)]
        return lax.ppermute(value, both, pairs)

    planes = jnp.asarray(cas_pair(np.arange(NX), np.arange(NX), NX)[0])
    split_z = np.concatenate([np.arange(0, NZ, 2), np.arange(1, NZ, 2)])
    fore = cas_pair(np.arange(NZ), split_z, NZ)
    back = cas_pair(split_z, np.arange(NZ), NZ)

    with jax.named_scope("pack"):
        payload = call(
            pack_kernel,
            (
                atom_count,
                base_index,
                fraction,
                charge.reshape(4, 128),
                owner_index.reshape(1, 128),
                neighbour,
            ),
            shape(56, 128),
            (
                pltpu.VMEM((3, 512), jnp.int32),
                pltpu.VMEM((3, 512), F32),
                pltpu.VMEM((4, 128), F32),
                pltpu.VMEM((1, 128), jnp.int32),
                pltpu.VMEM((NEIGH, 128), jnp.int32),
                pltpu.SemaphoreType.DMA((5,)),
            ),
            spaces={0: SM, 1: HB, 2: HB, 3: HB, 4: HB, 5: HB},
            limit=59,
        )
    with jax.named_scope("particles_in"):
        pair = lax.all_gather(payload, "core")
        far = [lax.ppermute(pair, both, chip_steps(kind)) for kind in range(3)]
        far = lax.all_gather(jnp.concatenate(far, axis=0), "core").reshape(12, 56, 128)
    place = (lax.axis_index("row") & 1) * 4 + lax.axis_index("core") * 2 + lax.axis_index("grp")
    where = place.astype(jnp.int32).reshape(1)
    with jax.named_scope("spread"):
        columns, part, h1, t2, to, beside, given = call(
            spread_kernel,
            (
                where,
                far,
                pair,
                layer_one.T,
                bias_one.reshape(1, -1),
                layer_two,
                bias_two.reshape(1, -1),
                layer_out.T,
                bias_out.reshape(1, -1),
                planes,
                influence,
            ),
            (
                shape(64, 2, 16, 128, dtype=BF),
                shape(6, ROWS, 128),
                shape(HID, 384),
                shape(HID, 384),
                shape(3, 384),
                shape(2, 56, 128),
                shape(128, 4, 256, dtype=BF),
            ),
            (
                pltpu.VMEM((14, 56, 128), F32),
                pltpu.VMEM((NEIGH, 8, 128), F32),
                pltpu.VMEM((24, 4, 8, 128), F32),
                pltpu.VMEM((128, 8, 128), F32),
                pltpu.VMEM((128, 768), BF),
                pltpu.VMEM((8, ROWS, 128), F32),
                pltpu.VMEM((8, ROWS, 128), F32),
                pltpu.VMEM((NX, 512), BF),
                pltpu.VMEM((NY, 512), BF),
                pltpu.VMEM((NX, 512), BF),
                pltpu.VMEM((NY, 512), BF),
                pltpu.VMEM((NX, NY), F32),
                pltpu.VMEM((NX, NX), BF),
                pltpu.VMEM((HID, 128), BF),
                pltpu.VMEM((1, HID), F32),
                pltpu.VMEM((HID, HID), BF),
                pltpu.VMEM((1, HID), F32),
                pltpu.VMEM((3, HID), BF),
                pltpu.VMEM((1, 3), F32),
                pltpu.VMEM((128, 4, 256), F32),
                pltpu.SemaphoreType.DMA((8,)),
            ),
            limit=58,
            spaces={0: SM, **{n: HB for n in range(3, 11)}},
            flops=4_000_000_000,
        )
    with jax.named_scope("influence_swap"):
        taken = lax.ppermute(given, "grp", [(0, 1), (1, 0)])
    with jax.named_scope("to_columns"):
        columns = lax.all_to_all(columns.reshape(256, 8, 128), both, 0, 0, tiled=True)
    def lookup(axis, kind):
        return call(
            lambda *refs: lookup_kernel(axis, kind, *refs),
            (part,),
            shape(22, NX, 256, dtype=kind),
            (pltpu.VMEM((4, ROWS, 128), F32), pltpu.VMEM((8, ROWS, 128), F32)),
            limit=58,
            flops=4_000_000_000,
        )

    with jax.named_scope("lookup_x"):
        weights_x = lookup(0, BF)
    with jax.named_scope("influence"):
        infl = call(
            influence_kernel,
            (where, influence, taken.astype(F32)),
            shape(NZ, 1024),
            spaces={0: SM},
        )
    with jax.named_scope("depth"):
        rows = call(
            depth_kernel,
            (
                columns.reshape(128, 16, 128),
                infl,
                jnp.asarray(np.stack(fore + back)),
            ),
            shape(128, 16, 128, dtype=BF),
            (
                pltpu.VMEM((128, 16, 128), F32),
                pltpu.VMEM((NZ, 1024), BF),
                pltpu.VMEM((128, 16, 128), F32),
            ),
            limit=50,
            flops=800_000_000,
        )
    with jax.named_scope("to_planes"):
        rows = lax.all_to_all(rows.reshape(256, 8, 128), both, 0, 0, tiled=True)
    with jax.named_scope("lookup_y"):
        weights_y = lookup(1, F32)
    with jax.named_scope("probe"):
        potential, *pushes = call(
            probe_kernel,
            (rows.reshape(64, 2, 16, 128), part, weights_x, weights_y, planes),
            (shape(1, NX, NY),) + (shape(ROWS, 128),) * 8,
            (
                pltpu.VMEM((NX, NY), BF),
                pltpu.VMEM((NY, NX), BF),
                pltpu.VMEM((NY, 256), F32),
                pltpu.VMEM((NY, 256), F32),
                pltpu.VMEM((3, ROWS, 128), F32),
                pltpu.VMEM((NX, NY), F32),
                pltpu.VMEM((22, NX, 256), BF),
                pltpu.VMEM((22, NY, 256), F32),
                pltpu.VMEM((NX, NX), BF),
                pltpu.SemaphoreType.DMA((5,)),
            ),
            first=HB,
            limit=52,
            spaces={2: HB, 3: HB, 4: HB},
            flops=5_000_000_000,
        )
    with jax.named_scope("pushes_out"):
        sums = [
            push if step == 0 else from_device(push, -step) for step, push in zip(NEAR, pushes)
        ]
    with jax.named_scope("force"):
        force = call(
            force_kernel,
            (*sums, beside, payload, h1, t2, to, layer_one.T, layer_two, layer_out.T),
            shape(3, 512),
            (pltpu.VMEM((128, 384), F32),),
            limit=16,
        )
    return force, potential


def solution(mesh):
    fine = Mesh(mesh.devices.reshape(64, 2, 2), ("row", "core", "grp"))
    return jax.shard_map(
        body,
        mesh=fine,
        in_specs=(
            P(None, ("row", "core", "grp")),
            P(None, ("row", "core", "grp")),
            P(("row", "core", "grp")),
            P(("row", "core", "grp")),
            P(("row", "core", "grp")),
            P(None, ("row", "core", "grp")),
            P("grp", ("row", "core"), None),
            P(),
            P(),
            P(),
            P(),
            P(),
            P(),
        ),
        out_specs=(P(None, ("row", "core", "grp")), P(("row", "core", "grp"), None, None)),
        check_vma=False,
    )
```

```python
import functools

import jax
import jax.numpy as jnp
import ml_dtypes
import numpy as np
from jax import lax
from jax.experimental import pallas as pl
from jax.experimental.pallas import tpu as pltpu
from jax.sharding import Mesh
from jax.sharding import PartitionSpec as P

NX = 512
NY = 512
NZ = 256
NEIGH = 32
HID = 240
CENTROID_CHARGE = -2.0
BF = jnp.bfloat16
F32 = jnp.float32
ROWS = 24
NEAR = tuple(range(-4, 4))
MIB = 1024 * 1024


def cas_pair(row_ids, column_ids, period):
    angle = 2.0 * np.pi / period * (np.outer(row_ids, column_ids) % period)
    table = np.cos(angle) + np.sin(angle)
    high = table.astype(ml_dtypes.bfloat16)
    low = (table - high.astype(np.float64)).astype(ml_dtypes.bfloat16)
    return high, low


def spline(offset):
    size = jnp.abs(offset)
    inner = 2.0 / 3.0 - size * size + 0.5 * size * size * size
    rest = 2.0 - size
    outer = rest * rest * rest * (1.0 / 6.0)
    return jnp.where(size < 1.0, inner, jnp.where(size < 2.0, outer, 0.0))


def spline_slope(offset):
    size = jnp.abs(offset)
    sign = jnp.where(offset > 0.0, 1.0, jnp.where(offset < 0.0, -1.0, 0.0))
    inner = (-2.0 * size + 1.5 * size * size) * sign
    rest = 2.0 - size
    outer = -0.5 * rest * rest * sign
    return jnp.where(size < 1.0, inner, jnp.where(size < 2.0, outer, 0.0))


def wrapped(values):
    return jnp.where(
        values >= 256.0, values - 512.0, jnp.where(values < -256.0, values + 512.0, values)
    )


def dot(left, right):
    return jnp.dot(left, right, preferred_element_type=F32)


def dot_first(left, right):
    return lax.dot_general(left, right, (((0,), (0,)), ((), ())), preferred_element_type=F32)


def split(values):
    high = values.astype(BF)
    low = (values - high.astype(F32)).astype(BF)
    return high, low


def chip_of(device):
    device = device % 256
    place = device % 8
    return device // 8 * 4 + place // 4 * 2 + place % 2, place // 2 % 2


def device_of(chip, core):
    chip = chip % 128
    return chip // 4 * 8 + chip % 4 // 2 * 4 + core * 2 + chip % 2


def chip_steps(kind):
    pairs = []
    for chip in range(128):
        if kind < 2:
            pairs.append((device_of(chip - kind - 1, 0), device_of(chip, 0)))
            pairs.append((device_of(chip + kind + 1, 1), device_of(chip, 1)))
        else:
            other = chip - 3 if chip % 2 else chip + 3
            pairs.append((device_of(other, 0), device_of(chip, 0)))
    return pairs


def row_index(place, step):
    there = place + step
    inner = there & 7
    chip = (there >> 3) * 4 + ((inner >> 2) & 1) * 2 + (inner & 1)
    away = chip - (((place >> 2) & 1) * 2 + (place & 1))
    first = jnp.where(away == 1, 6, jnp.where(away == 2, 8, 4))
    first = jnp.where(away == -1, 0, jnp.where(away == -2, 2, first))
    return jnp.where(away == 0, 12, first) + ((inner >> 1) & 1)


def fetch(pairs, sems, first=0):
    copies = [
        pltpu.make_async_copy(source, target, sems.at[first + n])
        for n, (source, target) in enumerate(pairs)
    ]
    for copy in copies:
        copy.start()
    return copies


def pack_kernel(
    count_ref, base_at, frac_at, charge_at, owner_at, near_at,
    out_ref, base_ref, frac_ref, charge_ref, owner_ref, near_ref, sems,
):
    arrays = (
        (base_at, base_ref), (frac_at, frac_ref), (charge_at, charge_ref),
        (owner_at, owner_ref), (near_at, near_ref),
    )
    copies = [pltpu.make_async_copy(a, b, sems.at[n]) for n, (a, b) in enumerate(arrays)]
    for copy in copies:
        copy.start()
    for copy in copies:
        copy.wait()
    for k in range(4):
        lanes = slice(128 * k, 128 * (k + 1))
        out_ref[k : k + 1, :] = base_ref[0:1, lanes].astype(F32)
        out_ref[4 + k : 5 + k, :] = base_ref[1:2, lanes].astype(F32)
        for c in range(3):
            out_ref[8 + 4 * c + k : 9 + 4 * c + k, :] = frac_ref[c : c + 1, lanes]
        slot = lax.broadcasted_iota(jnp.int32, (1, 128), 1) + 128 * k
        out_ref[20 + k : 21 + k, :] = jnp.where(
            slot < count_ref[0], charge_ref[k : k + 1, :], 0.0
        )
    owner = owner_ref[...]
    near = near_ref[...]
    side = jnp.where(near < 128, 0, jnp.where(near < 256, 8, 16))
    code = side + (((owner >> 4) - ((near & 127) >> 4)) & 7)
    atom = lax.broadcasted_iota(jnp.int32, (128, 128), 0)
    chosen = jnp.where(atom == owner, 1.0, 0.0).astype(BF)
    out_ref[24:56, :] = lax.dot_general(
        code.astype(F32).astype(BF), chosen, (((1,), (1,)), ((), ())), preferred_element_type=F32
    )


def atom_rows(part_ref, first, pay, plane):
    rows = slice(first, first + 4)
    for c in range(4):
        part_ref[c, rows, :] = pay(4 * c, 4 * c + 4)
    part_ref[4, rows, :] = plane - pay(16, 20)
    part_ref[5, rows, :] = pay(20, 24)


def stencil(base, frac):
    whole = jnp.floor(frac)
    cells, offsets = [], []
    for k in range(4):
        step = whole + float(k - 1)
        cell = base + step
        cell = jnp.where(cell < 0.0, cell + 512.0, jnp.where(cell >= 512.0, cell - 512.0, cell))
        cells.append(cell)
        offsets.append(step - frac)
    return cells, offsets


def densities(part_ref, cell_s, wgt_s, tables, total_s):
    charge_z = part_ref[5] * spline(part_ref[4])
    for axis in range(2):
        cells, offsets = stencil(part_ref[axis], part_ref[2 + axis])
        for k in range(4):
            value = spline(offsets[k])
            cell_s[axis * 4 + k] = cells[k]
            wgt_s[axis * 4 + k] = charge_z * value if axis == 0 else value
    place = lax.broadcasted_iota(jnp.int32, (16, 128), 0).astype(F32)
    zero = jnp.zeros((16, 128), BF)

    def fill(row, axis, table, lane):
        cells = [cell_s[axis * 4 + k, row : row + 1, :] for k in range(4)]
        blocks = [jnp.floor(cell * (1.0 / 16.0)) for cell in cells]
        here, there = jnp.zeros((16, 128), F32), jnp.zeros((16, 128), F32)
        for k in range(4):
            value = wgt_s[axis * 4 + k, row : row + 1, :]
            at = jnp.where(blocks[k] == blocks[0], cells[k] - 16.0 * blocks[k], -1.0)
            past = jnp.where(blocks[k] == blocks[0], -1.0, cells[k] - 16.0 * blocks[k])
            here = jnp.where(place == at, value, here)
            there = jnp.where(place == past, value, there)
        here, there = here.astype(BF), there.astype(BF)
        following = blocks[0] + 1.0
        following = jnp.where(following >= 32.0, 0.0, following)
        first = jnp.broadcast_to(blocks[0], (16, 128)).astype(BF)
        second = jnp.broadcast_to(following, (16, 128)).astype(BF)
        for part in range(32):
            label = jnp.full((16, 128), part, BF)
            table[16 * part : 16 * part + 16, lane : lane + 128] = jnp.where(
                first == label, here, jnp.where(second == label, there, zero)
            )

    def chunk(n):
        sx_s, wy_s = tables[n % 2]
        for m in range(4):
            fill(4 * n + m, 0, sx_s, 128 * m)
            fill(4 * n + m, 1, wy_s, 128 * m)

    def product(n):
        sx_s, wy_s = tables[n % 2]
        return lax.dot_general(
            sx_s[...], wy_s[...], (((1,), (1,)), ((), ())), preferred_element_type=F32
        )

    chunk(0)
    for n in range(6):
        if n < 5:
            chunk(n + 1)
        if n == 0:
            total_s[...] = product(n)
        elif n < 5:
            total_s[...] += product(n)
    return total_s[...] + product(5)


def spread_kernel(
    place_ref, far_ref, pair_ref,
    w1_at, b1_at, w2_at, b2_at, wo_at, bo_at, table_at, infl_at,
    out_ref, part_ref, h1_ref, t2_ref, to_ref, beside_ref, given_ref,
    rows_s, code_s, feat_s, in_s, xin_s, cell_s, wgt_s, sxa_s, wya_s, sxb_s, wyb_s, total_s,
    table_ref, w1_ref, b1_ref, w2_ref, b2_ref, wo_ref, bo_ref, half_s, sems,
):
    copies = fetch(
        (
            (w1_at, w1_ref), (b1_at, b1_ref), (w2_at, w2_ref),
            (b2_at, b2_ref), (wo_at, wo_ref), (bo_at, bo_ref),
        ),
        sems,
    )
    away = pl.multiple_of(256 - (place_ref[0] & 1) * 256, 256)
    table_copy, half_copy = fetch(
        ((table_at, table_ref), (infl_at.at[:, :, pl.ds(away, 256)], half_s)), sems, 6
    )
    index = [row_index(place_ref[0], step) for step in NEAR]
    rows_s[0:12] = far_ref[...]
    rows_s[12:14] = pair_ref[...]

    def pay(i, start, stop):
        return rows_s[index[i], start:stop, :]

    beside_ref[0] = pay(3, 0, 56)
    beside_ref[1] = pay(5, 0, 56)

    rim = [
        jnp.concatenate([pay(i, r, r + 1) for i in range(8)], axis=0) for r in (0, 4, 8, 12, 16)
    ]
    for i in range(8):
        code_s[:, i, :] = pay(i, 24, 56)
    for j in range(8):
        turned = [pltpu.roll(v, 16 * j, 1) if j else v for v in rim]
        for s in (-1, 0, 1):
            cand = [pltpu.roll(v, (-s) % 8, 0) if s else v for v in turned]
            dx = wrapped(cand[0] - rim[0]) + (cand[2] - rim[2])
            dy = wrapped(cand[1] - rim[1]) + (cand[3] - rim[3])
            dz = float(s) + (cand[4] - rim[4])
            scale = lax.rsqrt(1.0 + (dx * dx + dy * dy + dz * dz) * (1.0 / 16.0))
            c = (s + 1) * 8 + j
            feat_s[c, 0] = scale
            feat_s[c, 1] = scale * dx * 0.25
            feat_s[c, 2] = scale * dy * 0.25
            feat_s[c, 3] = scale * dz * 0.25

    def choose(block, carry):
        codes = [code_s[block * 4 + m] for m in range(4)]
        held = [[jnp.zeros((8, 128), F32) for _ in range(4)] for _ in range(4)]
        for c in range(24):
            feats = [feat_s[c, f] for f in range(4)]
            for m in range(4):
                mask = codes[m] == float(c)
                for f in range(4):
                    held[m][f] = jnp.where(mask, feats[f], held[m][f])
        for m in range(4):
            for f in range(4):
                in_s[(block * 4 + m) * 4 + f] = held[m][f]
        return carry

    lax.fori_loop(0, 8, choose, 0)
    for i in range(1, 7):
        xin_s[:, (i - 1) * 128 : i * 128] = in_s[:, i, :].astype(BF)
    for copy in copies:
        copy.wait()

    def column(row):
        wide = jnp.concatenate([row, jnp.zeros((1, 256 - row.shape[1]), F32)], axis=1)
        tall = jnp.broadcast_to(wide, (128, 256)).T[0 : row.shape[1]]
        return jnp.concatenate([tall] * 6, axis=1)

    h1 = jnp.tanh(dot(w1_ref[...], xin_s[...]) + column(b1_ref[...]))
    t2 = jnp.tanh(dot_first(w2_ref[...], h1.astype(BF)) + column(b2_ref[...]))
    to = jnp.tanh(dot(wo_ref[...], (t2 + h1).astype(BF)) + column(bo_ref[...]))
    h1_ref[...] = h1[:, 256:640]
    t2_ref[...] = t2[:, 256:640]
    to_ref[...] = to[:, 256:640]
    for n, i in enumerate((3, 4, 5, 2)):
        atom_rows(part_ref, 4 * n, lambda a, b, i=i: pay(i, a, b), float(4 - i))
    for i in range(1, 7):
        row = slice(15 + i, 16 + i)
        lanes = slice((i - 1) * 128, i * 128)
        part_ref[0, row, :] = pay(i, 0, 1)
        part_ref[1, row, :] = pay(i, 4, 5)
        part_ref[2, row, :] = pay(i, 8, 9) + to[0:1, lanes]
        part_ref[3, row, :] = pay(i, 12, 13) + to[1:2, lanes]
        part_ref[4, row, :] = float(4 - i) - (pay(i, 16, 17) + to[2:3, lanes])
        part_ref[5, row, :] = jnp.full((1, 128), CENTROID_CHARGE, F32)
    part_ref[:, 22:24, :] = jnp.zeros((6, 2, 128), F32)
    tables = ((sxa_s, wya_s), (sxb_s, wyb_s))
    density = densities(part_ref, cell_s, wgt_s, tables, total_s)
    half_copy.wait()
    given_ref[...] = half_s[...].astype(BF)
    table_copy.wait()
    hh = table_ref[...]
    high, low = split(density)
    inner = (dot(high, hh) + dot(low, hh)).astype(BF)
    spectrum = dot(hh, inner)
    lower = lax.broadcasted_iota(jnp.int32, (64, 8, 128), 1) < 4
    for g in range(2):
        tile0 = spectrum[:, 256 * g : 256 * g + 128].reshape(64, 8, 128)
        tile1 = spectrum[:, 256 * g + 128 : 256 * g + 256].reshape(64, 8, 128)
        even = jnp.where(lower, tile0, pltpu.roll(tile1, 4, 1))
        odd = jnp.where(lower, pltpu.roll(tile0, 4, 1), tile1)
        out_ref[:, 0, 8 * g : 8 * g + 8, :] = even.astype(BF)
        out_ref[:, 1, 8 * g : 8 * g + 8, :] = odd.astype(BF)


def influence_kernel(group_ref, kept_ref, taken_ref, out_ref):
    mine = pl.multiple_of((group_ref[0] & 1) * 128, 128)
    other = pl.multiple_of(128 - mine, 128)
    for r in range(8):
        lanes = slice(128 * r, 128 * r + 128)
        at = pl.multiple_of(2 * mine + 128 * (r // 4), 128)
        out_ref[pl.ds(mine, 128), lanes] = kept_ref[:, r % 4, pl.ds(at, 128)]
        out_ref[pl.ds(other, 128), lanes] = taken_ref[:, r % 4, 128 * (r // 4) : 128 * (r // 4) + 128]


def depth_kernel(
    x_ref, infl_ref, table_ref, out_ref, wide_s, xb_s, back_s
):
    wide_s[...] = x_ref[...].astype(F32)
    for r in range(8):
        lanes = slice(128 * r, 128 * r + 128)
        xb_s[0:128, lanes] = wide_s[:, r, :].astype(BF)
        xb_s[128:256, lanes] = wide_s[:, 8 + r, :].astype(BF)
    fh, fl, ih, il = (table_ref[n] for n in range(4))
    for r in range(0, 8, 2):
        lanes = slice(128 * r, 128 * r + 256)
        xb = xb_s[:, lanes]
        spectrum = dot(fh, xb) + dot(fl, xb)
        weighted = (spectrum * infl_ref[:, lanes]).astype(BF)
        back = dot(ih, weighted) + dot(il, weighted)
        for t in range(2):
            column = back[:, 128 * t : 128 * t + 128]
            back_s[:, r + t, :] = column[0:128]
            back_s[:, 8 + r + t, :] = column[128:256]
    out_ref[...] = back_s[...].astype(BF)


def cells_of(part_ref, cell_s, wgt_s, axes):
    for n, axis in enumerate(axes):
        cells, offsets = stencil(part_ref[axis], part_ref[2 + axis])
        for k in range(4):
            cell_s[n * 4 + k] = cells[k]
            wgt_s[n * 8 + k] = spline(offsets[k])
            wgt_s[n * 8 + 4 + k] = spline_slope(offsets[k])


def lookup_kernel(axis, kind, part_ref, out_ref, cell_s, wgt_s):
    cells_of(part_ref, cell_s, wgt_s, (axis,))

    def fill(row, carry):
        row_at = pl.ds(row, 1)
        cells = [cell_s[k, row_at, :] for k in range(4)]
        values = [wgt_s[k, row_at, :] for k in range(4)]
        slopes = [wgt_s[4 + k, row_at, :] for k in range(4)]
        for part in range(16):
            here = lax.broadcasted_iota(jnp.int32, (32, 128), 0).astype(F32) + 32.0 * part
            found = jnp.zeros((32, 128), F32)
            sloped = jnp.zeros((32, 128), F32)
            for k in range(4):
                mask = here == cells[k]
                found = jnp.where(mask, values[k], found)
                sloped = jnp.where(mask, slopes[k], sloped)
            out_ref[row, 32 * part : 32 * part + 32, 0:128] = found.astype(kind)
            out_ref[row, 32 * part : 32 * part + 32, 128:256] = sloped.astype(kind)
        return carry

    lax.fori_loop(0, 22, fill, 0)


def probe_kernel(
    y_ref, part_ref, wx_at, wy_at, table_at,
    pot_at, o0, o1, o2, o3, o4, o5, o6, o7,
    r_s, field_s, va_s, vb_s, push_s, pot_s, wx_ref, wy_ref, table_ref, sems,
):
    outs = (o0, o1, o2, o3, o4, o5, o6, o7)
    table_copy, wx_copy = fetch(((table_at, table_ref), (wx_at, wx_ref)), sems)
    lower = lax.broadcasted_iota(jnp.int32, (64, 8, 128), 1) < 4
    for g in range(2):
        even = y_ref[:, 0, 8 * g : 8 * g + 8, :].astype(F32)
        odd = y_ref[:, 1, 8 * g : 8 * g + 8, :].astype(F32)
        tile0 = jnp.where(lower, even, pltpu.roll(odd, 4, 1))
        tile1 = jnp.where(lower, pltpu.roll(even, 4, 1), odd)
        r_s[:, 256 * g : 256 * g + 128] = tile0.reshape(512, 128).astype(BF)
        r_s[:, 256 * g + 128 : 256 * g + 256] = tile1.reshape(512, 128).astype(BF)
    spans = ((0, 4), (4, 10), (10, 16), (16, 22))
    pieces = [pl.ds(first, last - first) for first, last in spans]
    wy_copies = fetch(tuple((wy_at.at[piece], wy_ref.at[piece]) for piece in pieces), sems, 3)
    table_copy.wait()
    hh = table_ref[...]
    inner = dot(hh, r_s[...])
    inner = inner.astype(BF)
    potential = dot(inner, hh) * (1.0 / 67108864.0)
    pot_s[...] = potential
    pot_copy = pltpu.make_async_copy(pot_s, pot_at.at[0], sems.at[2])
    pot_copy.start()
    field_s[...] = potential.T.astype(BF)


    def gather(row, vs_s):
        row_at = pl.ds(row, 1)
        probed = jnp.zeros((8, 128), F32)
        along_x = jnp.zeros((8, 128), F32)
        along_y = jnp.zeros((8, 128), F32)
        for part in range(64):
            rows = slice(8 * part, 8 * part + 8)
            found = wy_ref[row, rows, 0:128]
            value = vs_s[rows, 0:128]
            probed = probed + value * found
            along_x = along_x + vs_s[rows, 128:256] * found
            along_y = along_y + value * wy_ref[row, rows, 128:256]
        push_s[0, row_at, :] = jnp.sum(along_x, axis=0, keepdims=True)
        push_s[1, row_at, :] = jnp.sum(along_y, axis=0, keepdims=True)
        push_s[2, row_at, :] = jnp.sum(probed, axis=0, keepdims=True)

    def probe(pair, carry):
        row = 2 * pair
        vb_s[...] = dot(field_s[...], wx_ref[row + 1])
        gather(row, va_s)
        va_s[...] = dot(field_s[...], wx_ref[jnp.minimum(row + 2, 21)])
        gather(row + 1, vb_s)
        return carry

    wx_copy.wait()
    va_s[...] = dot(field_s[...], wx_ref[0])
    for (first, last), copy in zip(spans, wy_copies):
        copy.wait()
        lax.fori_loop(first // 2, last // 2, probe, 0)
    pot_copy.wait()
    charge = part_ref[5]
    charge_z = charge * spline(part_ref[4])
    charge_slope = charge * spline_slope(part_ref[4])
    push = [
        push_s[0] * charge_z,
        push_s[1] * charge_z,
        push_s[2] * charge_slope,
    ]
    for i, ref in enumerate(outs):
        ref[...] = jnp.zeros((ROWS, 128), F32)
        for c in range(3):
            if 2 <= i <= 5:
                first = (12, 0, 4, 8)[i - 2]
                ref[4 * c : 4 * c + 4, :] = push[c][first : first + 4]
            for m in range(3):
                source = i - 1 + m
                if 1 <= source <= 6:
                    to = 12 + 3 * c + m
                    ref[to : to + 1, :] = push[c][15 + source : 16 + source]


def force_kernel(
    s0, s1, s2, s3, s4, s5, s6, s7, beside_ref, own_ref,
    h1_ref, t2_ref, to_ref, w1_ref, w2_ref, wo_ref, out_ref, gin_s,
):
    total = s0[...] + s1[...] + s2[...] + s3[...] + s4[...] + s5[...] + s6[...] + s7[...]
    pull = [
        jnp.concatenate([total[12 + 3 * c + n : 13 + 3 * c + n] for n in range(3)], axis=1)
        for c in range(3)
    ]
    to = to_ref[...]
    g_out = jnp.concatenate(pull, axis=0) * (1.0 - to * to)
    g_two = dot_first(wo_ref[...], g_out.astype(BF))
    t2, h1 = t2_ref[...], h1_ref[...]
    g_pre = g_two * (1.0 - t2 * t2)
    g_one = dot(w2_ref[...], g_pre.astype(BF)) + g_two
    gin_s[...] = dot_first(w1_ref[...], (g_one * (1.0 - h1 * h1)).astype(BF))
    pays = (beside_ref.at[0], own_ref, beside_ref.at[1])
    turn = lax.broadcasted_iota(jnp.int32, (8, 128), 0).astype(F32)

    def rims(ref):
        return [ref[r : r + 1, :] for r in (0, 4, 8, 12, 16)]

    def rolled(row):
        return jnp.concatenate([pltpu.roll(row, 16 * j, 1) if j else row for j in range(8)], axis=0)

    own_rim = rims(own_ref)
    turned = [[rolled(row) for row in rims(ref)] for ref in pays]
    force = [total[4 * c : 4 * c + 1] for c in range(3)]
    owner_sum = [jnp.zeros((8, 128), F32) for _ in range(3)]
    for n, s in ((0, 1), (1, -1), (1, 0), (1, 1), (2, -1)):
        owner = rims(pays[n])
        cand = turned[n + s]
        dx = wrapped(cand[0] - owner[0]) + (cand[2] - owner[2])
        dy = wrapped(cand[1] - owner[1]) + (cand[3] - owner[3])
        dz = float(s) + (cand[4] - owner[4])
        scale = lax.rsqrt(1.0 + (dx * dx + dy * dy + dz * dz) * (1.0 / 16.0))
        lanes = slice(128 * n, 128 * n + 128)
        mine = turn + float(8 * (s + 1))
        cots = [jnp.zeros((8, 128), F32) for _ in range(4)]
        for m in range(NEIGH):
            mask = pays[n][24 + m : 25 + m, :] == mine
            for f in range(4):
                cots[f] = cots[f] + jnp.where(mask, gin_s[4 * m + f : 4 * m + f + 1, lanes], 0.0)
        along = cots[0] + (cots[1] * dx + cots[2] * dy + cots[3] * dz) * 0.25
        common = along * (scale * scale * scale) * (-1.0 / 16.0)
        moved = [
            common * dx + cots[1] * scale * 0.25,
            common * dy + cots[2] * scale * 0.25,
            common * dz + cots[3] * scale * 0.25,
        ]
        if n == 1:
            owner_sum = [owner_sum[c] + moved[c] for c in range(3)]
        if n + s == 1:
            for c in range(3):
                for j in range(8):
                    row = moved[c][j : j + 1]
                    force[c] = force[c] + (pltpu.roll(row, (-16 * j) % 128, 1) if j else row)
    for c in range(3):
        own = force[c] + pull[c][:, 128:256] - jnp.sum(owner_sum[c], axis=0, keepdims=True)
        out_ref[c : c + 1, 0:128] = own
        for k in range(1, 4):
            out_ref[c : c + 1, 128 * k : 128 * k + 128] = total[4 * c + k : 4 * c + k + 1]


VM = pl.BlockSpec(memory_space=pltpu.VMEM)


SM = pl.BlockSpec(memory_space=pltpu.SMEM)
HB = pl.BlockSpec(memory_space=pltpu.HBM)


def call(kernel, inputs, outs, scratch=(), limit=16, spaces=None, first=None, flops=0):
    spaces = spaces or {}
    out_specs = jax.tree.map(lambda _: VM, outs)
    if first is not None:
        out_specs = (first,) + tuple(out_specs)[1:]
    return pl.pallas_call(
        kernel,
        out_shape=outs,
        in_specs=[spaces.get(n, VM) for n in range(len(inputs))],
        out_specs=out_specs,
        scratch_shapes=list(scratch),
        compiler_params=pltpu.CompilerParams(vmem_limit_bytes=limit * MIB),
        cost_estimate=pl.CostEstimate(flops=flops, bytes_accessed=4 * MIB, transcendentals=0),
    )(*inputs)


def shape(*dims, dtype=F32):
    return jax.ShapeDtypeStruct(dims, dtype)


def body(
    base_index,
    fraction,
    charge,
    atom_count,
    owner_index,
    neighbour,
    influence,
    layer_one,
    bias_one,
    layer_two,
    bias_two,
    layer_out,
    bias_out,
):
    both = ("row", "core", "grp")
    devices = 256

    def from_device(value, step):
        pairs = [(source, (source - step) % devices) for source in range(devices)]
        return lax.ppermute(value, both, pairs)

    planes = jnp.asarray(cas_pair(np.arange(NX), np.arange(NX), NX)[0])
    split_z = np.concatenate([np.arange(0, NZ, 2), np.arange(1, NZ, 2)])
    fore = cas_pair(np.arange(NZ), split_z, NZ)
    back = cas_pair(split_z, np.arange(NZ), NZ)

    with jax.named_scope("pack"):
        payload = call(
            pack_kernel,
            (
                atom_count,
                base_index,
                fraction,
                charge.reshape(4, 128),
                owner_index.reshape(1, 128),
                neighbour,
            ),
            shape(56, 128),
            (
                pltpu.VMEM((3, 512), jnp.int32),
                pltpu.VMEM((3, 512), F32),
                pltpu.VMEM((4, 128), F32),
                pltpu.VMEM((1, 128), jnp.int32),
                pltpu.VMEM((NEIGH, 128), jnp.int32),
                pltpu.SemaphoreType.DMA((5,)),
            ),
            spaces={0: SM, 1: HB, 2: HB, 3: HB, 4: HB, 5: HB},
            limit=59,
        )
    with jax.named_scope("particles_in"):
        pair = lax.all_gather(payload, "core")
        far = [lax.ppermute(pair, both, chip_steps(kind)) for kind in range(3)]
        far = lax.all_gather(jnp.concatenate(far, axis=0), "core").reshape(12, 56, 128)
    place = (lax.axis_index("row") & 1) * 4 + lax.axis_index("core") * 2 + lax.axis_index("grp")
    where = place.astype(jnp.int32).reshape(1)
    with jax.named_scope("spread"):
        columns, part, h1, t2, to, beside, given = call(
            spread_kernel,
            (
                where,
                far,
                pair,
                layer_one.T,
                bias_one.reshape(1, -1),
                layer_two,
                bias_two.reshape(1, -1),
                layer_out.T,
                bias_out.reshape(1, -1),
                planes,
                influence,
            ),
            (
                shape(64, 2, 16, 128, dtype=BF),
                shape(6, ROWS, 128),
                shape(HID, 384),
                shape(HID, 384),
                shape(3, 384),
                shape(2, 56, 128),
                shape(128, 4, 256, dtype=BF),
            ),
            (
                pltpu.VMEM((14, 56, 128), F32),
                pltpu.VMEM((NEIGH, 8, 128), F32),
                pltpu.VMEM((24, 4, 8, 128), F32),
                pltpu.VMEM((128, 8, 128), F32),
                pltpu.VMEM((128, 768), BF),
                pltpu.VMEM((8, ROWS, 128), F32),
                pltpu.VMEM((8, ROWS, 128), F32),
                pltpu.VMEM((NX, 512), BF),
                pltpu.VMEM((NY, 512), BF),
                pltpu.VMEM((NX, 512), BF),
                pltpu.VMEM((NY, 512), BF),
                pltpu.VMEM((NX, NY), F32),
                pltpu.VMEM((NX, NX), BF),
                pltpu.VMEM((HID, 128), BF),
                pltpu.VMEM((1, HID), F32),
                pltpu.VMEM((HID, HID), BF),
                pltpu.VMEM((1, HID), F32),
                pltpu.VMEM((3, HID), BF),
                pltpu.VMEM((1, 3), F32),
                pltpu.VMEM((128, 4, 256), F32),
                pltpu.SemaphoreType.DMA((8,)),
            ),
            limit=58,
            spaces={0: SM, **{n: HB for n in range(3, 11)}},
            flops=4_000_000_000,
        )
    with jax.named_scope("influence_swap"):
        taken = lax.ppermute(given, "grp", [(0, 1), (1, 0)])
    with jax.named_scope("to_columns"):
        columns = lax.all_to_all(columns.reshape(256, 8, 128), both, 0, 0, tiled=True)
    def lookup(axis, kind):
        return call(
            lambda *refs: lookup_kernel(axis, kind, *refs),
            (part,),
            shape(22, NX, 256, dtype=kind),
            (pltpu.VMEM((4, ROWS, 128), F32), pltpu.VMEM((8, ROWS, 128), F32)),
            limit=58,
            flops=4_000_000_000,
        )

    with jax.named_scope("lookup_x"):
        weights_x = lookup(0, BF)
    with jax.named_scope("influence"):
        infl = call(
            influence_kernel,
            (where, influence, taken.astype(F32)),
            shape(NZ, 1024),
            spaces={0: SM},
        )
    with jax.named_scope("depth"):
        rows = call(
            depth_kernel,
            (
                columns.reshape(128, 16, 128),
                infl,
                jnp.asarray(np.stack(fore + back)),
            ),
            shape(128, 16, 128, dtype=BF),
            (
                pltpu.VMEM((128, 16, 128), F32),
                pltpu.VMEM((NZ, 1024), BF),
                pltpu.VMEM((128, 16, 128), F32),
            ),
            limit=50,
            flops=800_000_000,
        )
    with jax.named_scope("to_planes"):
        rows = lax.all_to_all(rows.reshape(256, 8, 128), both, 0, 0, tiled=True)
    with jax.named_scope("lookup_y"):
        weights_y = lookup(1, F32)
    with jax.named_scope("probe"):
        potential, *pushes = call(
            probe_kernel,
            (rows.reshape(64, 2, 16, 128), part, weights_x, weights_y, planes),
            (shape(1, NX, NY),) + (shape(ROWS, 128),) * 8,
            (
                pltpu.VMEM((NX, NY), BF),
                pltpu.VMEM((NY, NX), BF),
                pltpu.VMEM((NY, 256), F32),
                pltpu.VMEM((NY, 256), F32),
                pltpu.VMEM((3, ROWS, 128), F32),
                pltpu.VMEM((NX, NY), F32),
                pltpu.VMEM((22, NX, 256), BF),
                pltpu.VMEM((22, NY, 256), F32),
                pltpu.VMEM((NX, NX), BF),
                pltpu.SemaphoreType.DMA((7,)),
            ),
            first=HB,
            limit=52,
            spaces={2: HB, 3: HB, 4: HB},
            flops=5_000_000_000,
        )
    with jax.named_scope("pushes_out"):
        sums = [
            push if step == 0 else from_device(push, -step) for step, push in zip(NEAR, pushes)
        ]
    with jax.named_scope("force"):
        force = call(
            force_kernel,
            (*sums, beside, payload, h1, t2, to, layer_one.T, layer_two, layer_out.T),
            shape(3, 512),
            (pltpu.VMEM((128, 384), F32),),
            limit=16,
        )
    return force, potential


def solution(mesh):
    fine = Mesh(mesh.devices.reshape(64, 2, 2), ("row", "core", "grp"))
    return jax.shard_map(
        body,
        mesh=fine,
        in_specs=(
            P(None, ("row", "core", "grp")),
            P(None, ("row", "core", "grp")),
            P(("row", "core", "grp")),
            P(("row", "core", "grp")),
            P(("row", "core", "grp")),
            P(None, ("row", "core", "grp")),
            P("grp", ("row", "core"), None),
            P(),
            P(),
            P(),
            P(),
            P(),
            P(),
        ),
        out_specs=(P(None, ("row", "core", "grp")), P(("row", "core", "grp"), None, None)),
        check_vma=False,
    )
```

```python
import functools

import jax
import jax.numpy as jnp
import ml_dtypes
import numpy as np
from jax import lax
from jax.experimental import pallas as pl
from jax.experimental.pallas import tpu as pltpu
from jax.sharding import Mesh
from jax.sharding import PartitionSpec as P

NX = 512
NY = 512
NZ = 256
NEIGH = 32
HID = 240
CENTROID_CHARGE = -2.0
BF = jnp.bfloat16
F32 = jnp.float32
ROWS = 24
NEAR = tuple(range(-4, 4))
MIB = 1024 * 1024


def cas_pair(row_ids, column_ids, period):
    angle = 2.0 * np.pi / period * (np.outer(row_ids, column_ids) % period)
    table = np.cos(angle) + np.sin(angle)
    high = table.astype(ml_dtypes.bfloat16)
    low = (table - high.astype(np.float64)).astype(ml_dtypes.bfloat16)
    return high, low


def spline(offset):
    size = jnp.abs(offset)
    inner = 2.0 / 3.0 - size * size + 0.5 * size * size * size
    rest = 2.0 - size
    outer = rest * rest * rest * (1.0 / 6.0)
    return jnp.where(size < 1.0, inner, jnp.where(size < 2.0, outer, 0.0))


def spline_slope(offset):
    size = jnp.abs(offset)
    sign = jnp.where(offset > 0.0, 1.0, jnp.where(offset < 0.0, -1.0, 0.0))
    inner = (-2.0 * size + 1.5 * size * size) * sign
    rest = 2.0 - size
    outer = -0.5 * rest * rest * sign
    return jnp.where(size < 1.0, inner, jnp.where(size < 2.0, outer, 0.0))


def wrapped(values):
    return jnp.where(
        values >= 256.0, values - 512.0, jnp.where(values < -256.0, values + 512.0, values)
    )


def dot(left, right):
    return jnp.dot(left, right, preferred_element_type=F32)


def dot_first(left, right):
    return lax.dot_general(left, right, (((0,), (0,)), ((), ())), preferred_element_type=F32)


def split(values):
    high = values.astype(BF)
    low = (values - high.astype(F32)).astype(BF)
    return high, low


def chip_of(device):
    device = device % 256
    place = device % 8
    return device // 8 * 4 + place // 4 * 2 + place % 2, place // 2 % 2


def device_of(chip, core):
    chip = chip % 128
    return chip // 4 * 8 + chip % 4 // 2 * 4 + core * 2 + chip % 2


def chip_steps(kind):
    pairs = []
    for chip in range(128):
        if kind < 2:
            pairs.append((device_of(chip - kind - 1, 0), device_of(chip, 0)))
            pairs.append((device_of(chip + kind + 1, 1), device_of(chip, 1)))
        else:
            other = chip - 3 if chip % 2 else chip + 3
            pairs.append((device_of(other, 0), device_of(chip, 0)))
    return pairs


def row_index(place, step):
    there = place + step
    inner = there & 7
    chip = (there >> 3) * 4 + ((inner >> 2) & 1) * 2 + (inner & 1)
    away = chip - (((place >> 2) & 1) * 2 + (place & 1))
    first = jnp.where(away == 1, 6, jnp.where(away == 2, 8, 4))
    first = jnp.where(away == -1, 0, jnp.where(away == -2, 2, first))
    return jnp.where(away == 0, 12, first) + ((inner >> 1) & 1)


def fetch(pairs, sems, first=0):
    copies = [
        pltpu.make_async_copy(source, target, sems.at[first + n])
        for n, (source, target) in enumerate(pairs)
    ]
    for copy in copies:
        copy.start()
    return copies


def pack_kernel(
    count_at, base_at, frac_at, charge_at, owner_at, near_at,
    out_ref, count_ref, base_ref, frac_ref, charge_ref, owner_ref, near_ref, sems,
):
    arrays = (
        (base_at, base_ref), (frac_at, frac_ref), (charge_at, charge_ref),
        (owner_at, owner_ref), (near_at, near_ref), (count_at, count_ref),
    )
    copies = [pltpu.make_async_copy(a, b, sems.at[n]) for n, (a, b) in enumerate(arrays)]
    for copy in copies:
        copy.start()
    for copy in copies:
        copy.wait()
    for k in range(4):
        lanes = slice(128 * k, 128 * (k + 1))
        out_ref[k : k + 1, :] = base_ref[0:1, lanes].astype(F32)
        out_ref[4 + k : 5 + k, :] = base_ref[1:2, lanes].astype(F32)
        for c in range(3):
            out_ref[8 + 4 * c + k : 9 + 4 * c + k, :] = frac_ref[c : c + 1, lanes]
        slot = lax.broadcasted_iota(jnp.int32, (1, 128), 1) + 128 * k
        out_ref[20 + k : 21 + k, :] = jnp.where(
            slot < count_ref[...], charge_ref[k : k + 1, :], 0.0
        )
    owner = owner_ref[...]
    near = near_ref[...]
    side = jnp.where(near < 128, 0, jnp.where(near < 256, 8, 16))
    code = side + (((owner >> 4) - ((near & 127) >> 4)) & 7)
    atom = lax.broadcasted_iota(jnp.int32, (128, 128), 0)
    chosen = jnp.where(atom == owner, 1.0, 0.0).astype(BF)
    out_ref[24:56, :] = lax.dot_general(
        code.astype(F32).astype(BF), chosen, (((1,), (1,)), ((), ())), preferred_element_type=F32
    )


def atom_rows(part_ref, first, pay, plane):
    rows = slice(first, first + 4)
    for c in range(4):
        part_ref[c, rows, :] = pay(4 * c, 4 * c + 4)
    part_ref[4, rows, :] = plane - pay(16, 20)
    part_ref[5, rows, :] = pay(20, 24)


def stencil(base, frac):
    whole = jnp.floor(frac)
    cells, offsets = [], []
    for k in range(4):
        step = whole + float(k - 1)
        cell = base + step
        cell = jnp.where(cell < 0.0, cell + 512.0, jnp.where(cell >= 512.0, cell - 512.0, cell))
        cells.append(cell)
        offsets.append(step - frac)
    return cells, offsets


def densities(part_ref, cell_s, wgt_s, tables, total_s):
    charge_z = part_ref[5] * spline(part_ref[4])
    for axis in range(2):
        cells, offsets = stencil(part_ref[axis], part_ref[2 + axis])
        for k in range(4):
            value = spline(offsets[k])
            cell_s[axis * 4 + k] = cells[k]
            wgt_s[axis * 4 + k] = charge_z * value if axis == 0 else value
    place = lax.broadcasted_iota(jnp.int32, (16, 128), 0).astype(F32)
    zero = jnp.zeros((16, 128), BF)

    def fill(row, axis, table, lane):
        cells = [cell_s[axis * 4 + k, row : row + 1, :] for k in range(4)]
        blocks = [jnp.floor(cell * (1.0 / 16.0)) for cell in cells]
        here, there = jnp.zeros((16, 128), F32), jnp.zeros((16, 128), F32)
        for k in range(4):
            value = wgt_s[axis * 4 + k, row : row + 1, :]
            at = jnp.where(blocks[k] == blocks[0], cells[k] - 16.0 * blocks[k], -1.0)
            past = jnp.where(blocks[k] == blocks[0], -1.0, cells[k] - 16.0 * blocks[k])
            here = jnp.where(place == at, value, here)
            there = jnp.where(place == past, value, there)
        here, there = here.astype(BF), there.astype(BF)
        following = blocks[0] + 1.0
        following = jnp.where(following >= 32.0, 0.0, following)
        first = jnp.broadcast_to(blocks[0], (16, 128)).astype(BF)
        second = jnp.broadcast_to(following, (16, 128)).astype(BF)
        for part in range(32):
            label = jnp.full((16, 128), part, BF)
            table[16 * part : 16 * part + 16, lane : lane + 128] = jnp.where(
                first == label, here, jnp.where(second == label, there, zero)
            )

    def chunk(n):
        sx_s, wy_s = tables[n % 2]
        for m in range(4):
            fill(4 * n + m, 0, sx_s, 128 * m)
            fill(4 * n + m, 1, wy_s, 128 * m)

    def product(n):
        sx_s, wy_s = tables[n % 2]
        return lax.dot_general(
            sx_s[...], wy_s[...], (((1,), (1,)), ((), ())), preferred_element_type=F32
        )

    chunk(0)
    for n in range(6):
        if n < 5:
            chunk(n + 1)
        if n == 0:
            total_s[...] = product(n)
        elif n < 5:
            total_s[...] += product(n)
    return total_s[...] + product(5)


def spread_kernel(
    place_ref, far_ref, pair_ref,
    w1_at, b1_at, w2_at, b2_at, wo_at, bo_at, table_at, infl_at,
    out_ref, part_ref, h1_ref, t2_ref, to_ref, beside_ref, given_ref,
    rows_s, code_s, feat_s, in_s, xin_s, cell_s, wgt_s, sxa_s, wya_s, sxb_s, wyb_s, total_s,
    table_ref, w1_ref, b1_ref, w2_ref, b2_ref, wo_ref, bo_ref, half_s, sems,
):
    copies = fetch(
        (
            (w1_at, w1_ref), (b1_at, b1_ref), (w2_at, w2_ref),
            (b2_at, b2_ref), (wo_at, wo_ref), (bo_at, bo_ref),
        ),
        sems,
    )
    away = pl.multiple_of(256 - (place_ref[0] & 1) * 256, 256)
    table_copy, half_copy = fetch(
        ((table_at, table_ref), (infl_at.at[:, :, pl.ds(away, 256)], half_s)), sems, 6
    )
    index = [row_index(place_ref[0], step) for step in NEAR]
    rows_s[0:12] = far_ref[...]
    rows_s[12:14] = pair_ref[...]

    def pay(i, start, stop):
        return rows_s[index[i], start:stop, :]

    beside_ref[0] = pay(3, 0, 56)
    beside_ref[1] = pay(5, 0, 56)

    rim = [
        jnp.concatenate([pay(i, r, r + 1) for i in range(8)], axis=0) for r in (0, 4, 8, 12, 16)
    ]
    for i in range(8):
        code_s[:, i, :] = pay(i, 24, 56)
    for j in range(8):
        turned = [pltpu.roll(v, 16 * j, 1) if j else v for v in rim]
        for s in (-1, 0, 1):
            cand = [pltpu.roll(v, (-s) % 8, 0) if s else v for v in turned]
            dx = wrapped(cand[0] - rim[0]) + (cand[2] - rim[2])
            dy = wrapped(cand[1] - rim[1]) + (cand[3] - rim[3])
            dz = float(s) + (cand[4] - rim[4])
            scale = lax.rsqrt(1.0 + (dx * dx + dy * dy + dz * dz) * (1.0 / 16.0))
            c = (s + 1) * 8 + j
            feat_s[c, 0] = scale
            feat_s[c, 1] = scale * dx * 0.25
            feat_s[c, 2] = scale * dy * 0.25
            feat_s[c, 3] = scale * dz * 0.25

    def choose(block, carry):
        codes = [code_s[block * 4 + m] for m in range(4)]
        held = [[jnp.zeros((8, 128), F32) for _ in range(4)] for _ in range(4)]
        for c in range(24):
            feats = [feat_s[c, f] for f in range(4)]
            for m in range(4):
                mask = codes[m] == float(c)
                for f in range(4):
                    held[m][f] = jnp.where(mask, feats[f], held[m][f])
        for m in range(4):
            for f in range(4):
                in_s[(block * 4 + m) * 4 + f] = held[m][f]
        return carry

    lax.fori_loop(0, 8, choose, 0)
    for i in range(1, 7):
        xin_s[:, (i - 1) * 128 : i * 128] = in_s[:, i, :].astype(BF)
    for copy in copies:
        copy.wait()

    def column(row):
        wide = jnp.concatenate([row, jnp.zeros((1, 256 - row.shape[1]), F32)], axis=1)
        tall = jnp.broadcast_to(wide, (128, 256)).T[0 : row.shape[1]]
        return jnp.concatenate([tall] * 6, axis=1)

    h1 = jnp.tanh(dot(w1_ref[...], xin_s[...]) + column(b1_ref[...]))
    t2 = jnp.tanh(dot_first(w2_ref[...], h1.astype(BF)) + column(b2_ref[...]))
    to = jnp.tanh(dot(wo_ref[...], (t2 + h1).astype(BF)) + column(bo_ref[...]))
    h1_ref[...] = h1[:, 256:640]
    t2_ref[...] = t2[:, 256:640]
    to_ref[...] = to[:, 256:640]
    for n, i in enumerate((3, 4, 5, 2)):
        atom_rows(part_ref, 4 * n, lambda a, b, i=i: pay(i, a, b), float(4 - i))
    for i in range(1, 7):
        row = slice(15 + i, 16 + i)
        lanes = slice((i - 1) * 128, i * 128)
        part_ref[0, row, :] = pay(i, 0, 1)
        part_ref[1, row, :] = pay(i, 4, 5)
        part_ref[2, row, :] = pay(i, 8, 9) + to[0:1, lanes]
        part_ref[3, row, :] = pay(i, 12, 13) + to[1:2, lanes]
        part_ref[4, row, :] = float(4 - i) - (pay(i, 16, 17) + to[2:3, lanes])
        part_ref[5, row, :] = jnp.full((1, 128), CENTROID_CHARGE, F32)
    part_ref[:, 22:24, :] = jnp.zeros((6, 2, 128), F32)
    tables = ((sxa_s, wya_s), (sxb_s, wyb_s))
    density = densities(part_ref, cell_s, wgt_s, tables, total_s)
    half_copy.wait()
    given_ref[...] = half_s[...].astype(BF)
    table_copy.wait()
    hh = table_ref[...]
    high, low = split(density)
    inner = (dot(high, hh) + dot(low, hh)).astype(BF)
    spectrum = dot(hh, inner)
    lower = lax.broadcasted_iota(jnp.int32, (64, 8, 128), 1) < 4
    for g in range(2):
        tile0 = spectrum[:, 256 * g : 256 * g + 128].reshape(64, 8, 128)
        tile1 = spectrum[:, 256 * g + 128 : 256 * g + 256].reshape(64, 8, 128)
        even = jnp.where(lower, tile0, pltpu.roll(tile1, 4, 1))
        odd = jnp.where(lower, pltpu.roll(tile0, 4, 1), tile1)
        out_ref[:, 0, 8 * g : 8 * g + 8, :] = even.astype(BF)
        out_ref[:, 1, 8 * g : 8 * g + 8, :] = odd.astype(BF)


def influence_kernel(group_ref, kept_ref, taken_ref, out_ref):
    mine = pl.multiple_of((group_ref[0] & 1) * 128, 128)
    other = pl.multiple_of(128 - mine, 128)
    for r in range(8):
        lanes = slice(128 * r, 128 * r + 128)
        at = pl.multiple_of(2 * mine + 128 * (r // 4), 128)
        out_ref[pl.ds(mine, 128), lanes] = kept_ref[:, r % 4, pl.ds(at, 128)]
        out_ref[pl.ds(other, 128), lanes] = taken_ref[:, r % 4, 128 * (r // 4) : 128 * (r // 4) + 128]


def depth_kernel(
    x_ref, infl_ref, table_ref, out_ref, wide_s, xb_s, back_s
):
    wide_s[...] = x_ref[...].astype(F32)
    for r in range(8):
        lanes = slice(128 * r, 128 * r + 128)
        xb_s[0:128, lanes] = wide_s[:, r, :].astype(BF)
        xb_s[128:256, lanes] = wide_s[:, 8 + r, :].astype(BF)
    fh, fl, ih, il = (table_ref[n] for n in range(4))
    for r in range(0, 8, 2):
        lanes = slice(128 * r, 128 * r + 256)
        xb = xb_s[:, lanes]
        spectrum = dot(fh, xb) + dot(fl, xb)
        weighted = (spectrum * infl_ref[:, lanes]).astype(BF)
        back = dot(ih, weighted) + dot(il, weighted)
        for t in range(2):
            column = back[:, 128 * t : 128 * t + 128]
            back_s[:, r + t, :] = column[0:128]
            back_s[:, 8 + r + t, :] = column[128:256]
    out_ref[...] = back_s[...].astype(BF)


def cells_of(part_ref, cell_s, wgt_s, axes):
    for n, axis in enumerate(axes):
        cells, offsets = stencil(part_ref[axis], part_ref[2 + axis])
        for k in range(4):
            cell_s[n * 4 + k] = cells[k]
            wgt_s[n * 8 + k] = spline(offsets[k])
            wgt_s[n * 8 + 4 + k] = spline_slope(offsets[k])


def lookup_kernel(axis, kind, part_ref, out_ref, cell_s, wgt_s):
    cells_of(part_ref, cell_s, wgt_s, (axis,))

    def fill(row, carry):
        row_at = pl.ds(row, 1)
        cells = [cell_s[k, row_at, :] for k in range(4)]
        values = [wgt_s[k, row_at, :] for k in range(4)]
        slopes = [wgt_s[4 + k, row_at, :] for k in range(4)]
        for part in range(16):
            here = lax.broadcasted_iota(jnp.int32, (32, 128), 0).astype(F32) + 32.0 * part
            found = jnp.zeros((32, 128), F32)
            sloped = jnp.zeros((32, 128), F32)
            for k in range(4):
                mask = here == cells[k]
                found = jnp.where(mask, values[k], found)
                sloped = jnp.where(mask, slopes[k], sloped)
            out_ref[row, 32 * part : 32 * part + 32, 0:128] = found.astype(kind)
            out_ref[row, 32 * part : 32 * part + 32, 128:256] = sloped.astype(kind)
        return carry

    lax.fori_loop(0, 22, fill, 0)


def probe_kernel(
    y_ref, part_ref, wx_at, wy_at, table_at,
    pot_at, o0, o1, o2, o3, o4, o5, o6, o7,
    r_s, field_s, va_s, vb_s, push_s, pot_s, wx_ref, wy_ref, table_ref, sems,
):
    outs = (o0, o1, o2, o3, o4, o5, o6, o7)
    table_copy, wx_copy = fetch(((table_at, table_ref), (wx_at, wx_ref)), sems)
    lower = lax.broadcasted_iota(jnp.int32, (64, 8, 128), 1) < 4
    for g in range(2):
        even = y_ref[:, 0, 8 * g : 8 * g + 8, :].astype(F32)
        odd = y_ref[:, 1, 8 * g : 8 * g + 8, :].astype(F32)
        tile0 = jnp.where(lower, even, pltpu.roll(odd, 4, 1))
        tile1 = jnp.where(lower, pltpu.roll(even, 4, 1), odd)
        r_s[:, 256 * g : 256 * g + 128] = tile0.reshape(512, 128).astype(BF)
        r_s[:, 256 * g + 128 : 256 * g + 256] = tile1.reshape(512, 128).astype(BF)
    spans = ((0, 4), (4, 10), (10, 16), (16, 22))
    pieces = [pl.ds(first, last - first) for first, last in spans]
    wy_copies = fetch(tuple((wy_at.at[piece], wy_ref.at[piece]) for piece in pieces), sems, 3)
    table_copy.wait()
    hh = table_ref[...]
    inner = dot(hh, r_s[...])
    inner = inner.astype(BF)
    potential = dot(inner, hh) * (1.0 / 67108864.0)
    pot_s[...] = potential
    pot_copy = pltpu.make_async_copy(pot_s, pot_at.at[0], sems.at[2])
    pot_copy.start()
    field_s[...] = potential.T.astype(BF)


    def gather(row, vs_s):
        row_at = pl.ds(row, 1)
        probed = jnp.zeros((8, 128), F32)
        along_x = jnp.zeros((8, 128), F32)
        along_y = jnp.zeros((8, 128), F32)
        for part in range(64):
            rows = slice(8 * part, 8 * part + 8)
            found = wy_ref[row, rows, 0:128]
            value = vs_s[rows, 0:128]
            probed = probed + value * found
            along_x = along_x + vs_s[rows, 128:256] * found
            along_y = along_y + value * wy_ref[row, rows, 128:256]
        push_s[0, row_at, :] = jnp.sum(along_x, axis=0, keepdims=True)
        push_s[1, row_at, :] = jnp.sum(along_y, axis=0, keepdims=True)
        push_s[2, row_at, :] = jnp.sum(probed, axis=0, keepdims=True)

    def probe(pair, carry):
        row = 2 * pair
        vb_s[...] = dot(field_s[...], wx_ref[row + 1])
        gather(row, va_s)
        va_s[...] = dot(field_s[...], wx_ref[jnp.minimum(row + 2, 21)])
        gather(row + 1, vb_s)
        return carry

    wx_copy.wait()
    va_s[...] = dot(field_s[...], wx_ref[0])
    for (first, last), copy in zip(spans, wy_copies):
        copy.wait()
        lax.fori_loop(first // 2, last // 2, probe, 0)
    pot_copy.wait()
    charge = part_ref[5]
    charge_z = charge * spline(part_ref[4])
    charge_slope = charge * spline_slope(part_ref[4])
    push = [
        push_s[0] * charge_z,
        push_s[1] * charge_z,
        push_s[2] * charge_slope,
    ]
    for i, ref in enumerate(outs):
        ref[...] = jnp.zeros((ROWS, 128), F32)
        for c in range(3):
            if 2 <= i <= 5:
                first = (12, 0, 4, 8)[i - 2]
                ref[4 * c : 4 * c + 4, :] = push[c][first : first + 4]
            for m in range(3):
                source = i - 1 + m
                if 1 <= source <= 6:
                    to = 12 + 3 * c + m
                    ref[to : to + 1, :] = push[c][15 + source : 16 + source]


def force_kernel(
    s0, s1, s2, s3, s4, s5, s6, s7, beside_ref, own_ref,
    h1_ref, t2_ref, to_ref, w1_ref, w2_ref, wo_ref, out_ref, gin_s,
):
    total = s0[...] + s1[...] + s2[...] + s3[...] + s4[...] + s5[...] + s6[...] + s7[...]
    pull = [
        jnp.concatenate([total[12 + 3 * c + n : 13 + 3 * c + n] for n in range(3)], axis=1)
        for c in range(3)
    ]
    to = to_ref[...]
    g_out = jnp.concatenate(pull, axis=0) * (1.0 - to * to)
    g_two = dot_first(wo_ref[...], g_out.astype(BF))
    t2, h1 = t2_ref[...], h1_ref[...]
    g_pre = g_two * (1.0 - t2 * t2)
    g_one = dot(w2_ref[...], g_pre.astype(BF)) + g_two
    gin_s[...] = dot_first(w1_ref[...], (g_one * (1.0 - h1 * h1)).astype(BF))
    pays = (beside_ref.at[0], own_ref, beside_ref.at[1])
    turn = lax.broadcasted_iota(jnp.int32, (8, 128), 0).astype(F32)

    def rims(ref):
        return [ref[r : r + 1, :] for r in (0, 4, 8, 12, 16)]

    def rolled(row):
        return jnp.concatenate([pltpu.roll(row, 16 * j, 1) if j else row for j in range(8)], axis=0)

    own_rim = rims(own_ref)
    turned = [[rolled(row) for row in rims(ref)] for ref in pays]
    force = [total[4 * c : 4 * c + 1] for c in range(3)]
    owner_sum = [jnp.zeros((8, 128), F32) for _ in range(3)]
    for n, s in ((0, 1), (1, -1), (1, 0), (1, 1), (2, -1)):
        owner = rims(pays[n])
        cand = turned[n + s]
        dx = wrapped(cand[0] - owner[0]) + (cand[2] - owner[2])
        dy = wrapped(cand[1] - owner[1]) + (cand[3] - owner[3])
        dz = float(s) + (cand[4] - owner[4])
        scale = lax.rsqrt(1.0 + (dx * dx + dy * dy + dz * dz) * (1.0 / 16.0))
        lanes = slice(128 * n, 128 * n + 128)
        mine = turn + float(8 * (s + 1))
        cots = [jnp.zeros((8, 128), F32) for _ in range(4)]
        for m in range(NEIGH):
            mask = pays[n][24 + m : 25 + m, :] == mine
            for f in range(4):
                cots[f] = cots[f] + jnp.where(mask, gin_s[4 * m + f : 4 * m + f + 1, lanes], 0.0)
        along = cots[0] + (cots[1] * dx + cots[2] * dy + cots[3] * dz) * 0.25
        common = along * (scale * scale * scale) * (-1.0 / 16.0)
        moved = [
            common * dx + cots[1] * scale * 0.25,
            common * dy + cots[2] * scale * 0.25,
            common * dz + cots[3] * scale * 0.25,
        ]
        if n == 1:
            owner_sum = [owner_sum[c] + moved[c] for c in range(3)]
        if n + s == 1:
            for c in range(3):
                for j in range(8):
                    row = moved[c][j : j + 1]
                    force[c] = force[c] + (pltpu.roll(row, (-16 * j) % 128, 1) if j else row)
    for c in range(3):
        own = force[c] + pull[c][:, 128:256] - jnp.sum(owner_sum[c], axis=0, keepdims=True)
        out_ref[c : c + 1, 0:128] = own
        for k in range(1, 4):
            out_ref[c : c + 1, 128 * k : 128 * k + 128] = total[4 * c + k : 4 * c + k + 1]


VM = pl.BlockSpec(memory_space=pltpu.VMEM)


SM = pl.BlockSpec(memory_space=pltpu.SMEM)
HB = pl.BlockSpec(memory_space=pltpu.HBM)


def call(kernel, inputs, outs, scratch=(), limit=16, spaces=None, first=None, flops=0):
    spaces = spaces or {}
    out_specs = jax.tree.map(lambda _: VM, outs)
    if first is not None:
        out_specs = (first,) + tuple(out_specs)[1:]
    return pl.pallas_call(
        kernel,
        out_shape=outs,
        in_specs=[spaces.get(n, VM) for n in range(len(inputs))],
        out_specs=out_specs,
        scratch_shapes=list(scratch),
        compiler_params=pltpu.CompilerParams(vmem_limit_bytes=limit * MIB),
        cost_estimate=pl.CostEstimate(flops=flops, bytes_accessed=4 * MIB, transcendentals=0),
    )(*inputs)


def shape(*dims, dtype=F32):
    return jax.ShapeDtypeStruct(dims, dtype)


def body(
    base_index,
    fraction,
    charge,
    atom_count,
    owner_index,
    neighbour,
    influence,
    layer_one,
    bias_one,
    layer_two,
    bias_two,
    layer_out,
    bias_out,
):
    both = ("row", "core", "grp")
    devices = 256

    def from_device(value, step):
        pairs = [(source, (source - step) % devices) for source in range(devices)]
        return lax.ppermute(value, both, pairs)

    planes = jnp.asarray(cas_pair(np.arange(NX), np.arange(NX), NX)[0])
    split_z = np.concatenate([np.arange(0, NZ, 2), np.arange(1, NZ, 2)])
    fore = cas_pair(np.arange(NZ), split_z, NZ)
    back = cas_pair(split_z, np.arange(NZ), NZ)

    with jax.named_scope("pack"):
        payload = call(
            pack_kernel,
            (
                atom_count.reshape(1, 1),
                base_index,
                fraction,
                charge.reshape(4, 128),
                owner_index.reshape(1, 128),
                neighbour,
            ),
            shape(56, 128),
            (
                pltpu.VMEM((1, 1), jnp.int32),
                pltpu.VMEM((3, 512), jnp.int32),
                pltpu.VMEM((3, 512), F32),
                pltpu.VMEM((4, 128), F32),
                pltpu.VMEM((1, 128), jnp.int32),
                pltpu.VMEM((NEIGH, 128), jnp.int32),
                pltpu.SemaphoreType.DMA((6,)),
            ),
            spaces={n: HB for n in range(6)},
            limit=59,
        )
    with jax.named_scope("particles_in"):
        pair = lax.all_gather(payload, "core")
        far = [lax.ppermute(pair, both, chip_steps(kind)) for kind in range(3)]
        far = lax.all_gather(jnp.concatenate(far, axis=0), "core").reshape(12, 56, 128)
    place = (lax.axis_index("row") & 1) * 4 + lax.axis_index("core") * 2 + lax.axis_index("grp")
    where = place.astype(jnp.int32).reshape(1)
    with jax.named_scope("spread"):
        columns, part, h1, t2, to, beside, given = call(
            spread_kernel,
            (
                where,
                far,
                pair,
                layer_one.T,
                bias_one.reshape(1, -1),
                layer_two,
                bias_two.reshape(1, -1),
                layer_out.T,
                bias_out.reshape(1, -1),
                planes,
                influence,
            ),
            (
                shape(64, 2, 16, 128, dtype=BF),
                shape(6, ROWS, 128),
                shape(HID, 384),
                shape(HID, 384),
                shape(3, 384),
                shape(2, 56, 128),
                shape(128, 4, 256, dtype=BF),
            ),
            (
                pltpu.VMEM((14, 56, 128), F32),
                pltpu.VMEM((NEIGH, 8, 128), F32),
                pltpu.VMEM((24, 4, 8, 128), F32),
                pltpu.VMEM((128, 8, 128), F32),
                pltpu.VMEM((128, 768), BF),
                pltpu.VMEM((8, ROWS, 128), F32),
                pltpu.VMEM((8, ROWS, 128), F32),
                pltpu.VMEM((NX, 512), BF),
                pltpu.VMEM((NY, 512), BF),
                pltpu.VMEM((NX, 512), BF),
                pltpu.VMEM((NY, 512), BF),
                pltpu.VMEM((NX, NY), F32),
                pltpu.VMEM((NX, NX), BF),
                pltpu.VMEM((HID, 128), BF),
                pltpu.VMEM((1, HID), F32),
                pltpu.VMEM((HID, HID), BF),
                pltpu.VMEM((1, HID), F32),
                pltpu.VMEM((3, HID), BF),
                pltpu.VMEM((1, 3), F32),
                pltpu.VMEM((128, 4, 256), F32),
                pltpu.SemaphoreType.DMA((8,)),
            ),
            limit=58,
            spaces={0: SM, **{n: HB for n in range(3, 11)}},
            flops=4_000_000_000,
        )
    with jax.named_scope("influence_swap"):
        taken = lax.ppermute(given, "grp", [(0, 1), (1, 0)])
    with jax.named_scope("to_columns"):
        columns = lax.all_to_all(columns.reshape(256, 8, 128), both, 0, 0, tiled=True)
    def lookup(axis, kind):
        return call(
            lambda *refs: lookup_kernel(axis, kind, *refs),
            (part,),
            shape(22, NX, 256, dtype=kind),
            (pltpu.VMEM((4, ROWS, 128), F32), pltpu.VMEM((8, ROWS, 128), F32)),
            limit=58,
            flops=4_000_000_000,
        )

    with jax.named_scope("lookup_x"):
        weights_x = lookup(0, BF)
    with jax.named_scope("influence"):
        infl = call(
            influence_kernel,
            (where, influence, taken.astype(F32)),
            shape(NZ, 1024),
            spaces={0: SM},
        )
    with jax.named_scope("depth"):
        rows = call(
            depth_kernel,
            (
                columns.reshape(128, 16, 128),
                infl,
                jnp.asarray(np.stack(fore + back)),
            ),
            shape(128, 16, 128, dtype=BF),
            (
                pltpu.VMEM((128, 16, 128), F32),
                pltpu.VMEM((NZ, 1024), BF),
                pltpu.VMEM((128, 16, 128), F32),
            ),
            limit=50,
            flops=800_000_000,
        )
    with jax.named_scope("to_planes"):
        rows = lax.all_to_all(rows.reshape(256, 8, 128), both, 0, 0, tiled=True)
    with jax.named_scope("lookup_y"):
        weights_y = lookup(1, F32)
    with jax.named_scope("probe"):
        potential, *pushes = call(
            probe_kernel,
            (rows.reshape(64, 2, 16, 128), part, weights_x, weights_y, planes),
            (shape(1, NX, NY),) + (shape(ROWS, 128),) * 8,
            (
                pltpu.VMEM((NX, NY), BF),
                pltpu.VMEM((NY, NX), BF),
                pltpu.VMEM((NY, 256), F32),
                pltpu.VMEM((NY, 256), F32),
                pltpu.VMEM((3, ROWS, 128), F32),
                pltpu.VMEM((NX, NY), F32),
                pltpu.VMEM((22, NX, 256), BF),
                pltpu.VMEM((22, NY, 256), F32),
                pltpu.VMEM((NX, NX), BF),
                pltpu.SemaphoreType.DMA((7,)),
            ),
            first=HB,
            limit=52,
            spaces={2: HB, 3: HB, 4: HB},
            flops=5_000_000_000,
        )
    with jax.named_scope("pushes_out"):
        sums = [
            push if step == 0 else from_device(push, -step) for step, push in zip(NEAR, pushes)
        ]
    with jax.named_scope("force"):
        force = call(
            force_kernel,
            (*sums, beside, payload, h1, t2, to, layer_one.T, layer_two, layer_out.T),
            shape(3, 512),
            (pltpu.VMEM((128, 384), F32),),
            limit=16,
        )
    return force, potential


def solution(mesh):
    fine = Mesh(mesh.devices.reshape(64, 2, 2), ("row", "core", "grp"))
    return jax.shard_map(
        body,
        mesh=fine,
        in_specs=(
            P(None, ("row", "core", "grp")),
            P(None, ("row", "core", "grp")),
            P(("row", "core", "grp")),
            P(("row", "core", "grp")),
            P(("row", "core", "grp")),
            P(None, ("row", "core", "grp")),
            P("grp", ("row", "core"), None),
            P(),
            P(),
            P(),
            P(),
            P(),
            P(),
        ),
        out_specs=(P(None, ("row", "core", "grp")), P(("row", "core", "grp"), None, None)),
        check_vma=False,
    )
```
